128 devices in a mesh: group: 4 (over y), col: 32 (over z, x, core).
Axes of the slice: x: 4, y: 4, z: 4, core: 2. Of those that a mesh axis runs over, the one named last changes fastest.
Arguments:
- layer_input: bfloat16 [16384, 4096], P(('group', 'col')), may hold values from -6 to 6
- norm_gain: bfloat16 [4096], replicated, may hold values from 0.099609375 to 1.8984375
- keyvalue_cotangent: bfloat16 [16384, 2048], P(('group', 'col')), may hold values from -6 to 6
- keyvalue_weight: bfloat16 [4096, 2048], P('col'), may hold values from -0.125 to 0.125
- residual_cotangent: bfloat16 [16384, 4096], P(('group', 'col')), may hold values from -6 to 6
- ngram_ids: int32 [16384, 2], P(('group', 'col')), may hold values from 0 to 32767, as said below
- table: float32 [32768, 4096], P('group', 'col'), may hold values from -6 to 6
- accumulator: float32 [32768], P('group'), may hold values from 0.05 to 2
Outputs:
- new_table: float32 [32768, 4096], P('group', 'col')
- new_accum: float32 [32768], P('group')
The draws below stay inside these ranges and needn't reach their ends.
Inputs may be any that keep to these rules, and one draw needn't show every extreme that they name: `ngram_ids`: row r belongs to owner group r // 8192. Among the 256 entries of one device's tokens (aligned blocks of 128 tokens), at most 128 belong to any one owner group, and one owner group, the same for every device, holds exactly 128 of them.
All inputs are finite; a program needn't handle non-finite values.
Results may differ from the reference program's by a relative error of at most 0.0009.
Values may be sent and summed in bfloat16 or wider, within the bound.
No kernel may reach another device: no remote copies, remote signals or barrier semaphores. Data moves between devices by JAX's collectives and lax.ppermute only.
A program may use at most 128 MiB of HBM per device.

```python
import math
import jax
import jax.numpy as jnp
from jax import lax

D = 4096
KV = 1024
NGRAM = 2
TOK_DEV = 128
R_GRP = 8192
TOKENS = 16384
ROWS = 32768
N_GROUP = 4


def draw_ngram_ids(key, part):
    key = jax.random.fold_in(key, 5)
    keys = jax.random.split(key, 6)
    devices = TOKENS // TOK_DEV
    entries = TOK_DEV * NGRAM
    hottest = jax.random.randint(keys[0], (), 0, N_GROUP)
    device_keys = jax.random.split(keys[1], devices)
    orders = jax.vmap(lambda k: jax.random.permutation(k, entries))(device_keys)
    others = (hottest + 1 + jax.random.randint(keys[2], (devices, entries), 0, N_GROUP - 1)) % N_GROUP
    owners = jnp.where(orders < TOK_DEV, hottest, others)
    popular = jax.random.randint(keys[3], (devices, entries), 0, 4) == 0
    common_rows = jax.random.randint(keys[4], (devices, entries), 0, 32)
    spread_rows = jax.random.randint(keys[5], (devices, entries), 0, R_GRP)
    rows = jnp.where(popular, common_rows, spread_rows)
    return (owners * R_GRP + rows).astype(jnp.int32).reshape(TOKENS, NGRAM)


def steps_of(key, dims, shards, least, largest):
    loudness, own = 1.0, jax.random.fold_in(key, 6)
    for dim, blocks in shards:
        steps = jnp.exp(jax.random.uniform(jax.random.fold_in(own, dim), (blocks,), jnp.float32, least / len(shards), largest / len(shards)))
        loudness = loudness * jnp.repeat(steps, dims[dim] // blocks).reshape([-1 if axis == dim else 1 for axis in range(len(dims))])
    return loudness


def centred(own_key, shape, scale, limit, shards=(), kind=jnp.bfloat16):
    values = scale * jax.random.normal(own_key, shape, jnp.float32)
    if shards:
        values = values * steps_of(own_key, shape, shards, -0.22, 0.18)
    return jnp.clip(values, -limit, limit).astype(kind)


def setup_inputs(seed: int = 0) -> dict:
    key_list = jax.random.split(jax.random.key(seed), 9)
    layer_input = centred(key_list[0], (TOKENS, D), 1.0, 6.0, ((0, 128),))
    norm_gain = jnp.clip(1.0 + 0.18 * jax.random.normal(key_list[1], (D,), jnp.float32), 0.099609375, 1.8984375).astype(jnp.bfloat16)
    keyvalue_cotangent = centred(key_list[2], (TOKENS, 2 * KV), 1.0, 6.0, ((0, 128),))
    keyvalue_weight = centred(key_list[3], (D, 2 * KV), (2 * KV) ** -0.5, 0.125, ((0, 32),))
    residual_cotangent = centred(key_list[4], (TOKENS, D), 1.0, 6.0, ((0, 128),))
    ngram_ids = draw_ngram_ids(jax.random.fold_in(key_list[8], 71), 0)
    table = centred(key_list[6], (ROWS, D), 1.0, 6.0, ((0, 4), (1, 32)), jnp.float32)
    accumulator = jnp.clip(jnp.exp(math.log(2.0) - 3.6888794 * jax.random.uniform(key_list[7], (ROWS,), jnp.float32) ** steps_of(key_list[7], (ROWS,), ((0, 4),), -0.2, 0.2)), 0.05, 2.0)
    return dict(layer_input=layer_input, norm_gain=norm_gain, keyvalue_cotangent=keyvalue_cotangent, keyvalue_weight=keyvalue_weight, residual_cotangent=residual_cotangent, ngram_ids=ngram_ids, table=table, accumulator=accumulator)


learn_rate = 0.5

def token_gradient(layer_input, norm_gain, keyvalue_cotangent, keyvalue_weight, residual_cotangent):
    values = layer_input.astype(jnp.float32)
    inverse = lax.rsqrt(lax.optimization_barrier(jnp.mean(values * values, axis=-1, keepdims=True)) + 1e-05)
    normed_grad = jnp.dot(keyvalue_cotangent, keyvalue_weight.T, preferred_element_type=jnp.float32)
    scaled = normed_grad * norm_gain.astype(jnp.float32)
    inner = lax.optimization_barrier(jnp.mean(scaled * values, axis=-1, keepdims=True))
    total = inverse * scaled - values * (inverse * inverse * inverse) * inner + residual_cotangent.astype(jnp.float32)
    return total.astype(jnp.bfloat16)

def leaders_of(ids):
    count = ids.shape[0]
    order = jnp.arange(count, dtype=jnp.int32)
    same = ids[:, None] == ids[None, :]
    return lax.optimization_barrier(jnp.min(jnp.where(same, order[None, :], count), axis=1)).astype(jnp.int32)

def reference(layer_input, norm_gain, keyvalue_cotangent, keyvalue_weight, residual_cotangent, ngram_ids, table, accumulator):
    block = TOK_DEV
    count = TOKENS // block
    entries = block * NGRAM

    def accumulate(carry, index):
        start = index * block
        piece_input = lax.dynamic_slice_in_dim(layer_input, start, block, 0)
        piece_cot = lax.dynamic_slice_in_dim(keyvalue_cotangent, start, block, 0)
        piece_res = lax.dynamic_slice_in_dim(residual_cotangent, start, block, 0)
        piece_ids = lax.dynamic_slice_in_dim(ngram_ids, start, block, 0).reshape(-1)
        rows = token_gradient(piece_input, norm_gain, piece_cot, keyvalue_weight, piece_res)
        spread = jnp.broadcast_to(rows[:, None, :], (block, NGRAM, D)).reshape(entries, D)
        leader = leaders_of(piece_ids)
        merged = jnp.zeros((entries, D), jnp.float32).at[leader].add(spread.astype(jnp.float32))
        merged = merged.astype(jnp.bfloat16)
        is_leader = leader == jnp.arange(entries, dtype=jnp.int32)
        targets = jnp.where(is_leader, piece_ids, ROWS).astype(jnp.int32)
        carry = carry.at[targets].add(merged.astype(jnp.float32), mode='drop')
        return (carry, None)
    gradient, unused = lax.scan(accumulate, jnp.zeros((ROWS, D), jnp.float32), jnp.arange(count, dtype=jnp.int32))
    squares = lax.optimization_barrier(jnp.sum(gradient * gradient, axis=1)) / D
    new_accum = accumulator + squares
    new_table = table - learn_rate * gradient * lax.rsqrt(new_accum)[:, None]
    return (new_table, new_accum)
```

```python
import functools

import jax
import jax.numpy as jnp
from jax import lax
from jax.experimental import pallas as pl
from jax.experimental.pallas import tpu as pltpu
from jax.sharding import PartitionSpec as P

NGRAM = 2
R_GRP = 8192
PAD = 8
VMEM_LIMIT = 56 * 1024 * 1024
learn_rate = 0.5

NT = (((1,), (1,)), ((), ()))
NN = (((1,), (0,)), ((), ()))


def slots_of(ngram_ids, groups):
    tok = ngram_ids.shape[0]
    ids = ngram_ids.reshape(-1)
    n = ids.shape[0]
    order = jnp.arange(n, dtype=jnp.int32)
    same = ids[:, None] == ids[None, :]
    leader = jnp.min(jnp.where(same, order[None, :], n), axis=1)
    lead = leader == order
    owner = ids // R_GRP
    before = lead[None, :] & (owner[:, None] == owner[None, :]) & (order[None, :] < leader[:, None])
    slot = owner * tok + jnp.sum(before.astype(jnp.int32), axis=1)
    places = jnp.arange(groups * tok, dtype=jnp.int32)
    rows = jnp.min(
        jnp.where(places[:, None] == slot[None, :], (ids - owner * R_GRP)[None, :], R_GRP), axis=1
    )
    return slot.reshape(tok, NGRAM).T, rows.reshape(groups, tok)


def grad_kernel(steps, per, groups, width, cot, w, v, r, gain, slot, out, ng, ss, inner, count):
    i = pl.program_id(0)
    tok = cot.shape[0]
    cols = w.shape[0]

    @pl.when(i == 0)
    def _():
        ss[...] = jnp.zeros_like(ss)
        inner[...] = jnp.zeros_like(inner)
        place = lax.broadcasted_iota(jnp.int32, count.shape, 0)
        total = (place == slot[0:1, :]).astype(jnp.float32)
        for j in range(1, NGRAM):
            total += (place == slot[j : j + 1, :]).astype(jnp.float32)
        count[...] = total.astype(count.dtype)

    @pl.when(i < steps)
    def _():
        at = pl.ds(pl.multiple_of(i * cols, cols), cols)
        part = lax.dot_general(cot[...], w[...], NT, preferred_element_type=jnp.float32)
        scaled = part * gain[:, at].astype(jnp.float32)
        ng[i] = scaled
        values = v[:, at].astype(jnp.float32)
        ss[...] += jnp.sum(values * values, axis=1, keepdims=True)
        inner[...] += jnp.sum(scaled * values, axis=1, keepdims=True)

    @pl.when(i >= steps)
    def _():
        inverse = lax.rsqrt(ss[...] / width + 1e-05)
        cubed = inverse * inverse * inverse
        mean = inner[...] / width
        for k in range(per):
            step = (i - steps) * per + k
            at = pl.ds(pl.multiple_of(step * cols, cols), cols)
            values = v[:, at].astype(jnp.float32)
            total = inverse * ng[step] - values * cubed * mean + r[:, at].astype(jnp.float32)
            merged = lax.dot_general(
                count[...], total.astype(jnp.bfloat16), NN, preferred_element_type=jnp.float32
            ).astype(jnp.bfloat16)
            lanes = out.shape[3]
            for g in range(groups):
                for c in range(cols // lanes):
                    out[g, k * (cols // lanes) + c] = merged[
                        g * tok : (g + 1) * tok, c * lanes : (c + 1) * lanes
                    ]


def merged_rows(cot, w, v, r, gain, slot, groups, columns, lanes):
    tok, width = v.shape
    cols, per = 2 * lanes, 2
    steps = width // cols
    last = steps // per
    whole = lambda i: (0, 0)
    return pl.pallas_call(
        functools.partial(grad_kernel, steps, per, groups, width),
        grid=(steps + last,),
        in_specs=[
            pl.BlockSpec(cot.shape, whole),
            pl.BlockSpec((cols, w.shape[1]), lambda i: (jnp.minimum(i, steps - 1), 0)),
            pl.BlockSpec(v.shape, whole),
            pl.BlockSpec(r.shape, whole),
            pl.BlockSpec((1, width), whole),
            pl.BlockSpec(slot.shape, whole),
        ],
        out_specs=pl.BlockSpec(
            (groups, per * cols // lanes, tok, lanes), lambda i: (0, jnp.maximum(i - steps, 0), 0, 0)
        ),
        out_shape=jax.ShapeDtypeStruct((groups, columns, tok, lanes), jnp.bfloat16),
        scratch_shapes=[
            pltpu.VMEM((steps, tok, cols), jnp.float32),
            pltpu.VMEM((tok, 1), jnp.float32),
            pltpu.VMEM((tok, 1), jnp.float32),
            pltpu.VMEM((groups * tok, tok), jnp.bfloat16),
        ],
        compiler_params=pltpu.CompilerParams(
            dimension_semantics=("arbitrary",), vmem_limit_bytes=VMEM_LIMIT
        ),
        name="grad_merge",
    )(cot, w, v, r, gain.reshape(1, width), slot)


def scatter_kernel(per, batch, rows, counts, x, grad, sq, wide):
    i = pl.program_id(0)
    tok = x.shape[1]

    @pl.when(i == 0)
    def _():
        grad[...] = jnp.zeros_like(grad)

    for k in range(per):
        wide[k] = x[k].astype(jnp.float32)

    def block(k, carry):
        b = i * per + k
        n = counts[b]

        def some(j, carry):
            base = j * batch
            at = [rows[b, base + s] for s in range(batch)]
            old = [grad[pl.ds(at[s], 1), :] for s in range(batch)]
            new = [old[s] + wide[k, pl.ds(base + s, 1), :] for s in range(batch)]
            for s in range(batch):
                grad[pl.ds(at[s], 1), :] = new[s]
            return carry

        return lax.fori_loop(0, (n + batch - 1) // batch, some, carry)

    lax.fori_loop(0, per, block, 0)

    @pl.when(i == pl.num_programs(0) - 1)
    def _():
        ones = jnp.ones((8, grad.shape[1]), jnp.float32)

        def sums(j, carry):
            g = grad[pl.ds(pl.multiple_of(j * tok, tok), tok), :]
            s = lax.dot_general(
                ones,
                g * g,
                NT,
                preferred_element_type=jnp.float32,
                precision=lax.Precision.HIGHEST,
            )
            sq[pl.ds(j, 1), :] = s[0:1, :]
            return carry

        lax.fori_loop(0, sq.shape[0], sums, 0)


def scattered(arrived, rows, counts):
    blocks, tok, lanes = arrived.shape
    per = 8
    return pl.pallas_call(
        functools.partial(scatter_kernel, per, 16),
        grid_spec=pltpu.PrefetchScalarGridSpec(
            num_scalar_prefetch=2,
            grid=(blocks // per,),
            in_specs=[pl.BlockSpec((per, tok, lanes), lambda i, *_: (i, 0, 0))],
            out_specs=[
                pl.BlockSpec((R_GRP + PAD, lanes), lambda i, *_: (0, 0)),
                pl.BlockSpec((R_GRP // lanes, lanes), lambda i, *_: (0, 0)),
            ],
            scratch_shapes=[pltpu.VMEM((per, tok, lanes), jnp.float32)],
        ),
        out_shape=[
            jax.ShapeDtypeStruct((R_GRP + PAD, lanes), jnp.float32),
            jax.ShapeDtypeStruct((R_GRP // lanes, lanes), jnp.float32),
        ],
        compiler_params=pltpu.CompilerParams(
            dimension_semantics=("arbitrary",), vmem_limit_bytes=VMEM_LIMIT
        ),
        name="scatter_rows",
    )(rows, counts, arrived)


def update_kernel(table, grad, scale, out):
    lanes = scale.shape[1]
    for j in range(scale.shape[0]):
        at = pl.ds(j * lanes, lanes)
        wide = jnp.transpose(jnp.broadcast_to(scale[j : j + 1, :], (lanes, lanes)))
        out[at, :] = table[at, :] - learn_rate * grad[at, :] * wide


def updated(table, grad, scale):
    rows, lanes = table.shape
    tile = 1024
    return pl.pallas_call(
        update_kernel,
        grid=(rows // tile,),
        in_specs=[
            pl.BlockSpec((tile, lanes), lambda i: (i, 0)),
            pl.BlockSpec((tile, lanes), lambda i: (i, 0)),
            pl.BlockSpec((tile // lanes, lanes), lambda i: (i, 0)),
        ],
        out_specs=pl.BlockSpec((tile, lanes), lambda i: (i, 0)),
        out_shape=jax.ShapeDtypeStruct(table.shape, table.dtype),
        compiler_params=pltpu.CompilerParams(dimension_semantics=("arbitrary",)),
        name="update_rows",
    )(table, grad, scale)


def col_sum(x):
    def shifted(value, inner_size, size, by):
        pairs = []
        for d in range(lax.axis_size("col")):
            low, high = d % inner_size, d // inner_size
            mid, top = high % size, high // size
            pairs.append((d, (top * size + (mid + by) % size) * inner_size + low))
        return lax.ppermute(value, "col", pairs)

    x = x + shifted(x, 1, 2, 1)
    for inner_size in (2, 8):
        first, second, third = (shifted(x, inner_size, 4, by) for by in (1, 3, 2))
        x = (x + third) + (first + second)
    return x


def shards(
    layer_input,
    norm_gain,
    keyvalue_cotangent,
    keyvalue_weight,
    residual_cotangent,
    ngram_ids,
    table,
    accumulator,
):
    groups, columns = lax.axis_size("group"), lax.axis_size("col")
    tok, width = layer_input.shape
    lanes = table.shape[1]
    weight = lax.all_gather(keyvalue_weight, "col", axis=0, tiled=True)
    slot, rows = slots_of(ngram_ids, groups)
    sent_rows = jnp.broadcast_to(rows[:, None, :], (groups, columns, tok))
    got_rows = lax.all_to_all(
        sent_rows.reshape(groups * columns, tok), ("group", "col"), 0, 0, tiled=True
    )
    counts = jnp.sum((got_rows < R_GRP).astype(jnp.int32), axis=1)
    merged = merged_rows(
        keyvalue_cotangent,
        weight,
        layer_input,
        residual_cotangent,
        norm_gain,
        slot,
        groups,
        columns,
        lanes,
    )
    arrived = lax.all_to_all(
        merged.reshape(groups * columns, tok, lanes), ("group", "col"), 0, 0, tiled=True
    )
    grad, partial = scattered(arrived, got_rows, counts)
    squares = col_sum(partial) / width
    new_accum = accumulator.reshape(squares.shape) + squares
    new_table = updated(table, grad, lax.rsqrt(new_accum))
    return (new_table, new_accum.reshape(-1))


def solution(mesh):
    in_specs = (
        P(("group", "col"), None),
        P(),
        P(("group", "col"), None),
        P("col", None),
        P(("group", "col"), None),
        P(("group", "col"), None),
        P("group", "col"),
        P("group"),
    )
    out_specs = (P("group", "col"), P("group"))
    return jax.shard_map(shards, mesh=mesh, in_specs=in_specs, out_specs=out_specs, check_vma=False)
```

```python
import functools

import jax
import jax.numpy as jnp
from jax import lax
from jax.experimental import pallas as pl
from jax.experimental.pallas import tpu as pltpu
from jax.sharding import PartitionSpec as P

NGRAM = 2
R_GRP = 8192
PAD = 8
VMEM_LIMIT = 56 * 1024 * 1024
learn_rate = 0.5

NT = (((1,), (1,)), ((), ()))
NN = (((1,), (0,)), ((), ()))


def slots_of(ngram_ids, groups):
    tok = ngram_ids.shape[0]
    ids = ngram_ids.reshape(-1)
    n = ids.shape[0]
    order = jnp.arange(n, dtype=jnp.int32)
    same = ids[:, None] == ids[None, :]
    leader = jnp.min(jnp.where(same, order[None, :], n), axis=1)
    lead = leader == order
    owner = ids // R_GRP
    before = lead[None, :] & (owner[:, None] == owner[None, :]) & (order[None, :] < leader[:, None])
    slot = owner * tok + jnp.sum(before.astype(jnp.int32), axis=1)
    places = jnp.arange(groups * tok, dtype=jnp.int32)
    rows = jnp.min(
        jnp.where(places[:, None] == slot[None, :], (ids - owner * R_GRP)[None, :], R_GRP), axis=1
    )
    return slot.reshape(tok, NGRAM).T, rows.reshape(groups, tok)


def grad_kernel(steps, per, groups, width, cot, w, v, r, gain, slot, out, ng, ss, inner, count):
    i = pl.program_id(0)
    tok = cot.shape[0]
    cols = w.shape[0]

    @pl.when(i == 0)
    def _():
        ss[...] = jnp.zeros_like(ss)
        inner[...] = jnp.zeros_like(inner)
        place = lax.broadcasted_iota(jnp.int32, count.shape, 0)
        total = (place == slot[0:1, :]).astype(jnp.float32)
        for j in range(1, NGRAM):
            total += (place == slot[j : j + 1, :]).astype(jnp.float32)
        count[...] = total.astype(count.dtype)

    @pl.when(i < steps)
    def _():
        at = pl.ds(pl.multiple_of(i * cols, cols), cols)
        part = lax.dot_general(cot[...], w[...], NT, preferred_element_type=jnp.float32)
        scaled = part * gain[:, at].astype(jnp.float32)
        ng[i] = scaled
        values = v[:, at].astype(jnp.float32)
        ss[...] += jnp.sum(values * values, axis=1, keepdims=True)
        inner[...] += jnp.sum(scaled * values, axis=1, keepdims=True)

    @pl.when(i >= steps)
    def _():
        inverse = lax.rsqrt(ss[...] / width + 1e-05)
        cubed = inverse * inverse * inverse
        mean = inner[...] / width
        for k in range(per):
            step = (i - steps) * per + k
            at = pl.ds(pl.multiple_of(step * cols, cols), cols)
            values = v[:, at].astype(jnp.float32)
            total = inverse * ng[step] - values * cubed * mean + r[:, at].astype(jnp.float32)
            merged = lax.dot_general(
                count[...], total.astype(jnp.bfloat16), NN, preferred_element_type=jnp.float32
            ).astype(jnp.bfloat16)
            lanes = out.shape[3]
            for g in range(groups):
                for c in range(cols // lanes):
                    out[g, k * (cols // lanes) + c] = merged[
                        g * tok : (g + 1) * tok, c * lanes : (c + 1) * lanes
                    ]


def merged_rows(cot, w, v, r, gain, slot, groups, columns, lanes):
    tok, width = v.shape
    cols, per = 2 * lanes, 2
    steps = width // cols
    last = steps // per
    whole = lambda i: (0, 0)
    return pl.pallas_call(
        functools.partial(grad_kernel, steps, per, groups, width),
        grid=(steps + last,),
        in_specs=[
            pl.BlockSpec(cot.shape, whole),
            pl.BlockSpec((cols, w.shape[1]), lambda i: (jnp.minimum(i, steps - 1), 0)),
            pl.BlockSpec(v.shape, whole),
            pl.BlockSpec(r.shape, whole),
            pl.BlockSpec((1, width), whole),
            pl.BlockSpec(slot.shape, whole),
        ],
        out_specs=pl.BlockSpec(
            (groups, per * cols // lanes, tok, lanes), lambda i: (0, jnp.maximum(i - steps, 0), 0, 0)
        ),
        out_shape=jax.ShapeDtypeStruct((groups, columns, tok, lanes), jnp.bfloat16),
        scratch_shapes=[
            pltpu.VMEM((steps, tok, cols), jnp.float32),
            pltpu.VMEM((tok, 1), jnp.float32),
            pltpu.VMEM((tok, 1), jnp.float32),
            pltpu.VMEM((groups * tok, tok), jnp.bfloat16),
        ],
        compiler_params=pltpu.CompilerParams(
            dimension_semantics=("arbitrary",), vmem_limit_bytes=VMEM_LIMIT
        ),
        name="grad_merge",
    )(cot, w, v, r, gain.reshape(1, width), slot)


def scatter_kernel(per, batch, rows, counts, x, grad, sq, wide):
    i = pl.program_id(0)
    tok = x.shape[1]

    @pl.when(i == 0)
    def _():
        grad[...] = jnp.zeros_like(grad)

    for k in range(per):
        wide[k] = x[k].astype(jnp.float32)

    def block(k, carry):
        b = i * per + k

        def part(low, high):
            for first in range(low, high, batch):
                at = [rows[b * tok + first + s] for s in range(batch)]
                old = [grad[pl.ds(at[s], 1), :] for s in range(batch)]
                new = [old[s] + wide[k, pl.ds(first + s, 1), :] for s in range(batch)]
                for s in range(batch):
                    grad[pl.ds(at[s], 1), :] = new[s]

        part(0, tok // 2)

        @pl.when(counts[b] > tok // 2)
        def _():
            part(tok // 2, tok)

        return carry

    lax.fori_loop(0, per, block, 0)

    @pl.when(i == pl.num_programs(0) - 1)
    def _():
        ones = jnp.ones((8, grad.shape[1]), jnp.float32)

        def sums(j, carry):
            g = grad[pl.ds(pl.multiple_of(j * tok, tok), tok), :]
            s = lax.dot_general(
                ones,
                g * g,
                NT,
                preferred_element_type=jnp.float32,
                precision=lax.Precision.HIGHEST,
            )
            sq[pl.ds(j, 1), :] = s[0:1, :]
            return carry

        lax.fori_loop(0, sq.shape[0], sums, 0)


def scattered(arrived, rows, counts):
    blocks, tok, lanes = arrived.shape
    per = 8
    return pl.pallas_call(
        functools.partial(scatter_kernel, per, 16),
        grid_spec=pltpu.PrefetchScalarGridSpec(
            num_scalar_prefetch=2,
            grid=(blocks // per,),
            in_specs=[pl.BlockSpec((per, tok, lanes), lambda i, *_: (i, 0, 0))],
            out_specs=[
                pl.BlockSpec((R_GRP + PAD, lanes), lambda i, *_: (0, 0)),
                pl.BlockSpec((R_GRP // lanes, lanes), lambda i, *_: (0, 0)),
            ],
            scratch_shapes=[pltpu.VMEM((per, tok, lanes), jnp.float32)],
        ),
        out_shape=[
            jax.ShapeDtypeStruct((R_GRP + PAD, lanes), jnp.float32),
            jax.ShapeDtypeStruct((R_GRP // lanes, lanes), jnp.float32),
        ],
        compiler_params=pltpu.CompilerParams(
            dimension_semantics=("arbitrary",), vmem_limit_bytes=VMEM_LIMIT
        ),
        name="scatter_rows",
    )(rows.reshape(-1), counts, arrived)


def update_kernel(table, grad, scale, out):
    lanes = scale.shape[1]
    for j in range(scale.shape[0]):
        at = pl.ds(j * lanes, lanes)
        wide = jnp.transpose(jnp.broadcast_to(scale[j : j + 1, :], (lanes, lanes)))
        out[at, :] = table[at, :] - learn_rate * grad[at, :] * wide


def updated(table, grad, scale):
    rows, lanes = table.shape
    tile = 1024
    return pl.pallas_call(
        update_kernel,
        grid=(rows // tile,),
        in_specs=[
            pl.BlockSpec((tile, lanes), lambda i: (i, 0)),
            pl.BlockSpec((tile, lanes), lambda i: (i, 0)),
            pl.BlockSpec((tile // lanes, lanes), lambda i: (i, 0)),
        ],
        out_specs=pl.BlockSpec((tile, lanes), lambda i: (i, 0)),
        out_shape=jax.ShapeDtypeStruct(table.shape, table.dtype),
        compiler_params=pltpu.CompilerParams(dimension_semantics=("arbitrary",)),
        name="update_rows",
    )(table, grad, scale)


def col_sum(x):
    def shifted(value, inner_size, size, by):
        pairs = []
        for d in range(lax.axis_size("col")):
            low, high = d % inner_size, d // inner_size
            mid, top = high % size, high // size
            pairs.append((d, (top * size + (mid + by) % size) * inner_size + low))
        return lax.ppermute(value, "col", pairs)

    x = x + shifted(x, 1, 2, 1)
    for inner_size in (2, 8):
        first, second, third = (shifted(x, inner_size, 4, by) for by in (1, 3, 2))
        x = (x + third) + (first + second)
    return x


def shards(
    layer_input,
    norm_gain,
    keyvalue_cotangent,
    keyvalue_weight,
    residual_cotangent,
    ngram_ids,
    table,
    accumulator,
):
    groups, columns = lax.axis_size("group"), lax.axis_size("col")
    tok, width = layer_input.shape
    lanes = table.shape[1]
    weight = lax.all_gather(keyvalue_weight, "col", axis=0, tiled=True)
    slot, rows = slots_of(ngram_ids, groups)
    sent_rows = jnp.broadcast_to(rows[:, None, :], (groups, columns, tok))
    got_rows = lax.all_to_all(
        sent_rows.reshape(groups * columns, tok), ("group", "col"), 0, 0, tiled=True
    )
    counts = jnp.sum((got_rows < R_GRP).astype(jnp.int32), axis=1)
    merged = merged_rows(
        keyvalue_cotangent,
        weight,
        layer_input,
        residual_cotangent,
        norm_gain,
        slot,
        groups,
        columns,
        lanes,
    )
    arrived = lax.all_to_all(
        merged.reshape(groups * columns, tok, lanes), ("group", "col"), 0, 0, tiled=True
    )
    grad, partial = scattered(arrived, got_rows, counts)
    squares = col_sum(partial) / width
    new_accum = accumulator.reshape(squares.shape) + squares
    new_table = updated(table, grad, lax.rsqrt(new_accum))
    return (new_table, new_accum.reshape(-1))


def solution(mesh):
    in_specs = (
        P(("group", "col"), None),
        P(),
        P(("group", "col"), None),
        P("col", None),
        P(("group", "col"), None),
        P(("group", "col"), None),
        P("group", "col"),
        P("group"),
    )
    out_specs = (P("group", "col"), P("group"))
    return jax.shard_map(shards, mesh=mesh, in_specs=in_specs, out_specs=out_specs, check_vma=False)
```

```python
import functools

import jax
import jax.numpy as jnp
from jax import lax
from jax.experimental import pallas as pl
from jax.experimental.pallas import tpu as pltpu
from jax.sharding import PartitionSpec as P

NGRAM = 2
R_GRP = 8192
PAD = 8
VMEM_LIMIT = 56 * 1024 * 1024
learn_rate = 0.5

NT = (((1,), (1,)), ((), ()))
NN = (((1,), (0,)), ((), ()))


def slots_of(ngram_ids, groups):
    tok = ngram_ids.shape[0]
    ids = ngram_ids.reshape(-1)
    n = ids.shape[0]
    order = jnp.arange(n, dtype=jnp.int32)
    same = ids[:, None] == ids[None, :]
    leader = jnp.min(jnp.where(same, order[None, :], n), axis=1)
    lead = leader == order
    owner = ids // R_GRP
    before = lead[None, :] & (owner[:, None] == owner[None, :]) & (order[None, :] < leader[:, None])
    slot = jnp.sum(before.astype(jnp.int32), axis=1)
    places = jnp.arange(groups * tok, dtype=jnp.int32)
    rows = jnp.min(
        jnp.where(
            places[:, None] == (owner * tok + slot)[None, :], (ids - owner * R_GRP)[None, :], R_GRP
        ),
        axis=1,
    )
    mine = owner[None, :] == jnp.arange(groups, dtype=jnp.int32)[:, None]
    maps = jnp.where(mine, slot[None, :], -1).reshape(groups, tok, NGRAM)
    parts = [rows.reshape(groups, tok)] + [maps[:, :, j] for j in range(NGRAM)]
    return jnp.concatenate(parts, axis=1)


def grad_kernel(steps, per, width, cot, w, v, r, gain, out, ng, ss, inner):
    i = pl.program_id(0)
    cols = w.shape[0]

    @pl.when(i == 0)
    def _():
        ss[...] = jnp.zeros_like(ss)
        inner[...] = jnp.zeros_like(inner)

    @pl.when(i < steps)
    def _():
        at = pl.ds(pl.multiple_of(i * cols, cols), cols)
        part = lax.dot_general(cot[...], w[...], NT, preferred_element_type=jnp.float32)
        scaled = part * gain[:, at].astype(jnp.float32)
        ng[i] = scaled
        values = v[:, at].astype(jnp.float32)
        ss[...] += jnp.sum(values * values, axis=1, keepdims=True)
        inner[...] += jnp.sum(scaled * values, axis=1, keepdims=True)

    @pl.when(i >= steps)
    def _():
        inverse = lax.rsqrt(ss[...] / width + 1e-05)
        cubed = inverse * inverse * inverse
        mean = inner[...] / width
        for k in range(per):
            step = (i - steps) * per + k
            at = pl.ds(pl.multiple_of(step * cols, cols), cols)
            values = v[:, at].astype(jnp.float32)
            total = inverse * ng[step] - values * cubed * mean + r[:, at].astype(jnp.float32)
            total = total.astype(jnp.bfloat16)
            lanes = out.shape[2]
            for c in range(cols // lanes):
                out[k * (cols // lanes) + c] = total[:, c * lanes : (c + 1) * lanes]


def token_grads(cot, w, v, r, gain, columns, lanes):
    tok, width = v.shape
    cols, per = 2 * lanes, 2
    steps = width // cols
    last = steps // per
    whole = lambda i: (0, 0)
    return pl.pallas_call(
        functools.partial(grad_kernel, steps, per, width),
        grid=(steps + last,),
        in_specs=[
            pl.BlockSpec(cot.shape, whole),
            pl.BlockSpec((cols, w.shape[1]), lambda i: (jnp.minimum(i, steps - 1), 0)),
            pl.BlockSpec(v.shape, whole),
            pl.BlockSpec(r.shape, whole),
            pl.BlockSpec((1, width), whole),
        ],
        out_specs=pl.BlockSpec(
            (per * cols // lanes, tok, lanes), lambda i: (jnp.maximum(i - steps, 0), 0, 0)
        ),
        out_shape=jax.ShapeDtypeStruct((columns, tok, lanes), jnp.bfloat16),
        scratch_shapes=[
            pltpu.VMEM((steps, tok, cols), jnp.float32),
            pltpu.VMEM((tok, 1), jnp.float32),
            pltpu.VMEM((tok, 1), jnp.float32),
        ],
        compiler_params=pltpu.CompilerParams(
            dimension_semantics=("arbitrary",), vmem_limit_bytes=VMEM_LIMIT
        ),
        name="token_grads",
    )(cot, w, v, r, gain.reshape(1, width))


def scatter_kernel(first, last, parts, per, batch, rows, counts, *refs):
    i = pl.program_id(0)
    n = len(parts)
    xs, maps = refs[:n], refs[n]
    if first:
        grad = refs[n + 1]
    else:
        held, grad = refs[n + 1], refs[n + 2]
    wide = refs[-1]
    tok, lanes = wide.shape[1], wide.shape[2]

    @pl.when(i == 0)
    def _():
        grad[...] = jnp.zeros_like(grad) if first else held[...]

    place = lax.broadcasted_iota(jnp.int32, (tok, tok), 0)

    def merge(x):
        for k in range(per):
            total = (place == maps[k, 0:1, :]).astype(jnp.float32)
            for j in range(1, NGRAM):
                total += (place == maps[k, j : j + 1, :]).astype(jnp.float32)
            wide[k] = (
                lax.dot_general(
                    total.astype(jnp.bfloat16), x[k], NN, preferred_element_type=jnp.float32
                )
                .astype(jnp.bfloat16)
                .astype(jnp.float32)
            )

    start = 0
    for p in range(n):
        pl.when((i >= start) & (i < start + parts[p]))(functools.partial(merge, xs[p]))
        start += parts[p]

    def block(k, carry):
        b = i * per + k

        def part(low, high):
            for base in range(low, high, batch):
                at = [rows[b * tok + base + s] for s in range(batch)]
                old = [grad[pl.ds(at[s], 1), :] for s in range(batch)]
                new = [old[s] + wide[k, pl.ds(base + s, 1), :] for s in range(batch)]
                for s in range(batch):
                    grad[pl.ds(at[s], 1), :] = new[s]

        part(0, tok // 2)

        @pl.when(counts[b] > tok // 2)
        def _():
            part(tok // 2, tok)

        return carry

    lax.fori_loop(0, per, block, 0)

    if last:
        sq = refs[n + 3]

        @pl.when(i == pl.num_programs(0) - 1)
        def _():
            ones = jnp.ones((8, lanes), jnp.float32)

            def sums(j, carry):
                g = grad[pl.ds(pl.multiple_of(j * tok, tok), tok), :]
                s = lax.dot_general(
                    ones,
                    g * g,
                    NT,
                    preferred_element_type=jnp.float32,
                    precision=lax.Precision.HIGHEST,
                )
                sq[pl.ds(j, 1), :] = s[0:1, :]
                return carry

            lax.fori_loop(0, sq.shape[0], sums, 0)


def scattered(xs, maps, rows, counts, held, last):
    tok, lanes = xs[0].shape[1:]
    per = 8
    parts = [x.shape[0] // per for x in xs]
    starts = [sum(parts[:p]) for p in range(len(parts))]

    def piece(p):
        return lambda i, *_: (jnp.clip(i - starts[p], 0, parts[p] - 1), 0, 0)

    total = (R_GRP + PAD, lanes)
    in_specs = [pl.BlockSpec((per, tok, lanes), piece(p)) for p in range(len(xs))]
    in_specs.append(pl.BlockSpec((per, NGRAM, tok), lambda i, *_: (i, 0, 0)))
    args = [rows.reshape(-1), counts, *xs, maps]
    whole = lambda i, *_: (0, 0)
    if held is not None:
        in_specs.append(pl.BlockSpec(total, whole))
        args.append(held)
    out_specs = [pl.BlockSpec(total, whole)]
    out_shape = [jax.ShapeDtypeStruct(total, jnp.float32)]
    if last:
        out_specs.append(pl.BlockSpec((R_GRP // lanes, lanes), whole))
        out_shape.append(jax.ShapeDtypeStruct((R_GRP // lanes, lanes), jnp.float32))
    return pl.pallas_call(
        functools.partial(scatter_kernel, held is None, last, parts, per, 16),
        grid_spec=pltpu.PrefetchScalarGridSpec(
            num_scalar_prefetch=2,
            grid=(sum(parts),),
            in_specs=in_specs,
            out_specs=out_specs,
            scratch_shapes=[pltpu.VMEM((per, tok, lanes), jnp.float32)],
        ),
        out_shape=out_shape,
        input_output_aliases={} if held is None else {len(args) - 1: 0},
        compiler_params=pltpu.CompilerParams(
            dimension_semantics=("arbitrary",), vmem_limit_bytes=28 * 1024 * 1024
        ),
        cost_estimate=pl.CostEstimate(
            flops=1000000, bytes_accessed=900000 * sum(x.shape[0] for x in xs), transcendentals=0
        ),
        name="scatter_rows",
    )(*args)


def ring(x, by):
    n = lax.axis_size("group")
    return lax.ppermute(x, "group", [(d, (d + by) % n) for d in range(n)])


def update_kernel(table, grad, scale, out):
    lanes = scale.shape[1]
    for j in range(scale.shape[0]):
        at = pl.ds(j * lanes, lanes)
        wide = jnp.transpose(jnp.broadcast_to(scale[j : j + 1, :], (lanes, lanes)))
        out[at, :] = table[at, :] - learn_rate * grad[at, :] * wide


def updated(table, grad, scale):
    rows, lanes = table.shape
    tile = 1024
    return pl.pallas_call(
        update_kernel,
        grid=(rows // tile,),
        in_specs=[
            pl.BlockSpec((tile, lanes), lambda i: (i, 0)),
            pl.BlockSpec((tile, lanes), lambda i: (i, 0)),
            pl.BlockSpec((tile // lanes, lanes), lambda i: (i, 0)),
        ],
        out_specs=pl.BlockSpec((tile, lanes), lambda i: (i, 0)),
        out_shape=jax.ShapeDtypeStruct(table.shape, table.dtype),
        compiler_params=pltpu.CompilerParams(dimension_semantics=("arbitrary",)),
        name="update_rows",
    )(table, grad, scale)


def col_sum(x):
    def shifted(value, inner_size, size, by):
        pairs = []
        for d in range(lax.axis_size("col")):
            low, high = d % inner_size, d // inner_size
            mid, top = high % size, high // size
            pairs.append((d, (top * size + (mid + by) % size) * inner_size + low))
        return lax.ppermute(value, "col", pairs)

    x = x + shifted(x, 1, 2, 1)
    for inner_size in (2, 8):
        first, second, third = (shifted(x, inner_size, 4, by) for by in (1, 3, 2))
        x = (x + third) + (first + second)
    return x


def shards(
    layer_input,
    norm_gain,
    keyvalue_cotangent,
    keyvalue_weight,
    residual_cotangent,
    ngram_ids,
    table,
    accumulator,
):
    groups, columns = lax.axis_size("group"), lax.axis_size("col")
    tok, width = layer_input.shape
    lanes = table.shape[1]
    weight = lax.all_gather(keyvalue_weight, "col", axis=0, tiled=True)
    plan = slots_of(ngram_ids, groups)
    sent = jnp.broadcast_to(plan[:, None, :], (groups, columns, plan.shape[1]))
    got = lax.all_to_all(
        sent.reshape(groups * columns, -1), ("group", "col"), 0, 0, tiled=True
    ).reshape(groups, columns, -1)
    me = lax.axis_index("group")
    got = [lax.dynamic_index_in_dim(got, (me + by) % groups, 0, False) for by in (0, 3, 1, 2)]
    got = [got[0], jnp.concatenate(got[1:3]), got[3]]
    rows = [g[:, :tok] for g in got]
    maps = [g[:, tok:].reshape(-1, NGRAM, tok) for g in got]
    counts = [jnp.sum((r < R_GRP).astype(jnp.int32), axis=1) for r in rows]
    cotangent, rows, maps, counts = lax.optimization_barrier(
        (keyvalue_cotangent, rows, maps, counts)
    )
    grads = token_grads(
        cotangent,
        weight,
        layer_input,
        residual_cotangent,
        norm_gain,
        columns,
        lanes,
    )
    own = lax.all_to_all(grads, "col", 0, 0, tiled=True)
    half = columns // 2
    left, right = ring(own, 1), ring(own, 3)
    (grad,) = scattered((own,), maps[0], rows[0], counts[0], None, False)
    left, right, grad = lax.optimization_barrier((left, right, grad))
    far = (ring(left[:half], 1), ring(right[half:], 3))
    (grad,) = scattered(
        (left, right),
        maps[1],
        rows[1],
        counts[1],
        grad,
        False,
    )
    grad, partial = scattered(far, maps[2], rows[2], counts[2], grad, True)
    squares = col_sum(partial) / width
    new_accum = accumulator.reshape(squares.shape) + squares
    new_table = updated(table, grad, lax.rsqrt(new_accum))
    return (new_table, new_accum.reshape(-1))


def solution(mesh):
    in_specs = (
        P(("group", "col"), None),
        P(),
        P(("group", "col"), None),
        P("col", None),
        P(("group", "col"), None),
        P(("group", "col"), None),
        P("group", "col"),
        P("group"),
    )
    out_specs = (P("group", "col"), P("group"))
    return jax.shard_map(shards, mesh=mesh, in_specs=in_specs, out_specs=out_specs, check_vma=False)
```

```python
import functools

import jax
import jax.numpy as jnp
from jax import lax
from jax.experimental import pallas as pl
from jax.experimental.pallas import tpu as pltpu
from jax.sharding import PartitionSpec as P

NGRAM = 2
R_GRP = 8192
PAD = 8
VMEM_LIMIT = 56 * 1024 * 1024
learn_rate = 0.5

NT = (((1,), (1,)), ((), ()))
NN = (((1,), (0,)), ((), ()))


def slots_of(ngram_ids, groups):
    tok = ngram_ids.shape[0]
    ids = ngram_ids.reshape(-1)
    n = ids.shape[0]
    order = jnp.arange(n, dtype=jnp.int32)
    same = ids[:, None] == ids[None, :]
    leader = jnp.min(jnp.where(same, order[None, :], n), axis=1)
    lead = leader == order
    owner = ids // R_GRP
    before = lead[None, :] & (owner[:, None] == owner[None, :]) & (order[None, :] < leader[:, None])
    slot = jnp.sum(before.astype(jnp.int32), axis=1)
    places = jnp.arange(groups * tok, dtype=jnp.int32)
    rows = jnp.min(
        jnp.where(
            places[:, None] == (owner * tok + slot)[None, :], (ids - owner * R_GRP)[None, :], R_GRP
        ),
        axis=1,
    )
    mine = owner[None, :] == jnp.arange(groups, dtype=jnp.int32)[:, None]
    maps = jnp.where(mine, slot[None, :], -1).reshape(groups, tok, NGRAM)
    parts = [rows.reshape(groups, tok)] + [maps[:, :, j] for j in range(NGRAM)]
    return jnp.concatenate(parts, axis=1)


def product_kernel(pieces, first, last, columns, *refs):
    n = len(pieces)
    where, refs = refs[0], refs[1:]
    cot_own, cot_pair = refs[0], refs[1]
    ws = refs[2 : 2 + n]
    tok, deep = cot_own.shape
    depth = deep // 2
    if first:
        v_own, v_pair, ng, ss = refs[2 + n :]
        ng[...] = jnp.zeros_like(ng)
    else:
        held, gain, v_own, v_pair, ng, inner = refs[2 + n :]
        ng[...] = held[...]
    lanes = ng.shape[3]
    for (half, blocks), w in zip(pieces, ws):
        at = slice(half * depth, (half + 1) * depth)
        for k in range(0, len(blocks), 2):
            rows = w[k * lanes : (k + 2) * lanes, :]
            for part, cot in enumerate((cot_own, cot_pair)):
                p = lax.dot_general(cot[:, at], rows, NT, preferred_element_type=jnp.float32)
                for j in range(2):
                    ng[blocks[k + j], part] += p[:, j * lanes : (j + 1) * lanes]
    if first:
        for part, v in enumerate((v_own, v_pair)):

            def squares(j, total):
                x = v[:, pl.ds(pl.multiple_of(j * lanes, lanes), lanes)].astype(jnp.float32)
                return total + x * x

            ss[part] = lax.fori_loop(0, columns, squares, jnp.zeros((tok, lanes), jnp.float32))
    if last:
        for part, v in enumerate((v_own, v_pair)):

            def products(j, total):
                at = pl.ds(pl.multiple_of(where[j] * lanes, lanes), lanes)
                scaled = ng[j, part] * gain[:, at].astype(jnp.float32)
                ng[j, part] = scaled
                return total + scaled * v[:, at].astype(jnp.float32)

            inner[part] = lax.fori_loop(
                0, ng.shape[0], products, jnp.zeros((tok, lanes), jnp.float32)
            )


def finish_kernel(width, where, ng, ss, inner, other, v_own, v_pair, r_own, r_pair, out):
    tok, lanes = ng.shape[2:]
    core = lax.rem(where[0], 2)
    for part, (v, r) in enumerate(((v_own, r_own), (v_pair, r_pair))):
        square = jnp.sum(ss[part], axis=1, keepdims=True)
        inverse = lax.rsqrt(square / width + 1e-05)
        cubed = inverse * inverse * inverse
        mean = jnp.sum(inner[part] + other[1 - part], axis=1, keepdims=True) / width
        place = core if part == 0 else 1 - core

        def block(j, carry):
            at = pl.ds(pl.multiple_of(where[j] * lanes, lanes), lanes)
            values = v[:, at].astype(jnp.float32)
            total = inverse * ng[j, part] - values * cubed * mean + r[:, at].astype(jnp.float32)
            out[lax.div(where[j], 2), place] = total.astype(out.dtype)
            return carry

        lax.fori_loop(0, ng.shape[0], block, 0)


def vmem_call(kernel, n, out_shape, name, aliases=None):
    space = pl.BlockSpec(memory_space=pltpu.VMEM)
    return pl.pallas_call(
        kernel,
        in_specs=[pl.BlockSpec(memory_space=pltpu.SMEM)] + [space] * (n - 1),
        out_specs=jax.tree.map(lambda _: space, out_shape),
        out_shape=out_shape,
        input_output_aliases=aliases or {},
        compiler_params=pltpu.CompilerParams(vmem_limit_bytes=40 * 1024 * 1024),
        name=name,
    )


def shifted(value, inner_size, size, by):
    pairs = []
    for d in range(lax.axis_size("col")):
        low, high = d % inner_size, d // inner_size
        mid, top = high % size, high // size
        pairs.append((d, (top * size + (mid + by) % size) * inner_size + low))
    return lax.ppermute(value, "col", pairs)


def along(x, axis):
    inner_size = {"x": 2, "z": 8}[axis]
    left, right = shifted(x, inner_size, 4, 1), shifted(x, inner_size, 4, 3)
    return left, right


def far_halves(left, right, axis):
    inner_size = {"x": 2, "z": 8}[axis]
    half = left.shape[0] // 2
    return shifted(left[:half], inner_size, 4, 1), shifted(right[half:], inner_size, 4, 3)


def token_grads(cot, w, v, r, gain, lanes):
    columns = lax.axis_size("col")
    tok, width = v.shape
    depth = w.shape[1] // 2
    me = lax.axis_index("col")
    z, x, core = me // 8, (me // 2) % 4, me % 2
    where = jnp.stack(
        [
            (((z + 4 - dz) % 4) * 4 + (x + 4 - dx) % 4) * 2 + core
            for dz in range(4)
            for dx in range(4)
        ]
    ).astype(jnp.int32)
    cot_pair, v_pair, r_pair = (shifted(t, 1, 2, 1) for t in (cot, v, r))
    rows = []
    for half, axis in enumerate("xz"):
        own = w[:, half * depth : (half + 1) * depth]
        left, right = along(own, axis)
        near, farther = far_halves(left, right, axis)
        rows.append(jnp.concatenate([own, left, near, farther, right]))
    sides = [along(rows[0], "z"), along(rows[1], "x")]
    far = [far_halves(*sides[0], "z"), far_halves(*sides[1], "x")]

    def line(half, k, low=0, high=4):
        return (half, [k * 4 + j if half == 0 else j * 4 + k for j in range(low, high)])

    pieces, ws = [], []
    for half in range(2):
        for k, piece in ((0, rows[half]), (1, sides[half][0]), (3, sides[half][1])):
            pieces.append(line(half, k))
            ws.append(piece)
    product = jax.ShapeDtypeStruct((16, 2, tok, lanes), jnp.float32)
    stat = jax.ShapeDtypeStruct((2, tok, lanes), jnp.float32)
    args = (where, cot, cot_pair, *ws, v, v_pair)
    ng, ss = vmem_call(
        functools.partial(product_kernel, pieces, True, False, columns),
        len(args),
        (product, stat),
        "product_near",
    )(*args)
    pieces, ws = [], []
    for half in range(2):
        for low, piece in ((0, far[half][0]), (2, far[half][1])):
            pieces.append(line(half, 2, low, low + 2))
            ws.append(piece)
    args = (where, cot, cot_pair, *ws, ng, gain.reshape(1, width), v, v_pair)
    scaled, inner = vmem_call(
        functools.partial(product_kernel, pieces, False, True, columns),
        len(args),
        (product, stat),
        "product_far",
        {len(args) - 4: 0},
    )(*args)
    other = shifted(inner, 1, 2, 1)
    args = (where, scaled, ss, inner, other, v, v_pair, r, r_pair)
    return vmem_call(
        functools.partial(finish_kernel, width),
        len(args),
        jax.ShapeDtypeStruct((16, 2, tok, lanes), jnp.bfloat16),
        "token_grads",
    )(*args)


def scatter_kernel(first, parts, per, batch, rows, counts, *refs):
    i = pl.program_id(0)
    n = len(parts)
    xs, maps = refs[:n], refs[n]
    if first:
        grad = refs[n + 1]
    else:
        held, grad = refs[n + 1], refs[n + 2]
    wide = refs[-1]
    tok, lanes = wide.shape[1], wide.shape[2]

    @pl.when(i == 0)
    def _():
        grad[...] = jnp.zeros_like(grad) if first else held[...]

    place = lax.broadcasted_iota(jnp.int32, (tok, tok), 0)

    def merge(x):
        for k in range(per):
            total = (place == maps[k, 0:1, :]).astype(jnp.float32)
            for j in range(1, NGRAM):
                total += (place == maps[k, j : j + 1, :]).astype(jnp.float32)
            wide[k] = (
                lax.dot_general(
                    total.astype(jnp.bfloat16), x[k], NN, preferred_element_type=jnp.float32
                )
                .astype(jnp.bfloat16)
                .astype(jnp.float32)
            )

    start = 0
    for p in range(n):
        pl.when((i >= start) & (i < start + parts[p]))(functools.partial(merge, xs[p]))
        start += parts[p]

    def block(k, carry):
        b = i * per + k

        def part(low, high):
            for base in range(low, high, batch):
                at = [rows[b * tok + base + s] for s in range(batch)]
                old = [grad[pl.ds(at[s], 1), :] for s in range(batch)]
                new = [old[s] + wide[k, pl.ds(base + s, 1), :] for s in range(batch)]
                for s in range(batch):
                    grad[pl.ds(at[s], 1), :] = new[s]

        part(0, tok // 2)

        @pl.when(counts[b] > tok // 2)
        def _():
            part(tok // 2, tok)

        return carry

    lax.fori_loop(0, per, block, 0)


def scattered(xs, maps, rows, counts, held):
    tok, lanes = xs[0].shape[1:]
    per = 8
    parts = [x.shape[0] // per for x in xs]
    starts = [sum(parts[:p]) for p in range(len(parts))]

    def piece(p):
        return lambda i, *_: (jnp.clip(i - starts[p], 0, parts[p] - 1), 0, 0)

    total = (R_GRP + PAD, lanes)
    in_specs = [pl.BlockSpec((per, tok, lanes), piece(p)) for p in range(len(xs))]
    in_specs.append(pl.BlockSpec((per, NGRAM, tok), lambda i, *_: (i, 0, 0)))
    args = [rows.reshape(-1), counts, *xs, maps]
    whole = lambda i, *_: (0, 0)
    if held is not None:
        in_specs.append(pl.BlockSpec(total, whole))
        args.append(held)
    return pl.pallas_call(
        functools.partial(scatter_kernel, held is None, parts, per, 16),
        grid_spec=pltpu.PrefetchScalarGridSpec(
            num_scalar_prefetch=2,
            grid=(sum(parts),),
            in_specs=in_specs,
            out_specs=pl.BlockSpec(total, whole),
            scratch_shapes=[pltpu.VMEM((per, tok, lanes), jnp.float32)],
        ),
        out_shape=jax.ShapeDtypeStruct(total, jnp.float32),
        input_output_aliases={} if held is None else {len(args) - 1: 0},
        compiler_params=pltpu.CompilerParams(
            dimension_semantics=("arbitrary",), vmem_limit_bytes=28 * 1024 * 1024
        ),
        cost_estimate=pl.CostEstimate(
            flops=1000000, bytes_accessed=900000 * sum(x.shape[0] for x in xs), transcendentals=0
        ),
        name="scatter_rows",
    )(*args)


def ring(x, by):
    n = lax.axis_size("group")
    return lax.ppermute(x, "group", [(d, (d + by) % n) for d in range(n)])


def col_sum(x):
    x = x + shifted(x, 1, 2, 1)
    for inner_size in (2, 8):
        first, second, third = (shifted(x, inner_size, 4, by) for by in (1, 3, 2))
        x = (x + third) + (first + second)
    return x


def shards(
    layer_input,
    norm_gain,
    keyvalue_cotangent,
    keyvalue_weight,
    residual_cotangent,
    ngram_ids,
    table,
    accumulator,
):
    groups, columns = lax.axis_size("group"), lax.axis_size("col")
    tok, width = layer_input.shape
    lanes = table.shape[1]
    plan = slots_of(ngram_ids, groups)
    sent = jnp.broadcast_to(plan[:, None, :], (groups, columns, plan.shape[1]))
    got = lax.all_to_all(
        sent.reshape(groups * columns, -1), ("group", "col"), 0, 0, tiled=True
    ).reshape(groups, columns, -1)
    me = lax.axis_index("group")
    got = [lax.dynamic_index_in_dim(got, (me + by) % groups, 0, False) for by in (0, 3, 1, 2)]
    got = [got[0], jnp.concatenate(got[1:3]), got[3]]
    rows = [g[:, :tok] for g in got]
    maps = [g[:, tok:].reshape(-1, NGRAM, tok) for g in got]
    counts = [jnp.sum((r < R_GRP).astype(jnp.int32), axis=1) for r in rows]
    cotangent, rows, maps, counts = lax.optimization_barrier(
        (keyvalue_cotangent, rows, maps, counts)
    )
    grads = token_grads(
        cotangent, keyvalue_weight, layer_input, residual_cotangent, norm_gain, lanes
    )
    planes = [[q * 2 + core for q in range(columns // 2)] for core in range(2)]
    own = lax.all_to_all(
        grads.reshape(columns // 2, 2 * tok, lanes),
        "col",
        0,
        0,
        axis_index_groups=planes,
        tiled=True,
    ).reshape(columns, tok, lanes)
    half = columns // 2
    left, right = ring(own, 1), ring(own, 3)
    grad = scattered((own,), maps[0], rows[0], counts[0], None)
    left, right, grad = lax.optimization_barrier((left, right, grad))
    far = (ring(left[:half], 1), ring(right[half:], 3))
    grad = scattered((left, right), maps[1], rows[1], counts[1], grad)
    grad = scattered(far, maps[2], rows[2], counts[2], grad)[:R_GRP]
    partial = jnp.sum(grad * grad, axis=1).reshape(-1, lanes)
    squares = col_sum(partial) / width
    new_accum = accumulator + squares.reshape(-1)
    new_table = table - learn_rate * grad * lax.rsqrt(new_accum)[:, None]
    return (new_table, new_accum)


def solution(mesh):
    in_specs = (
        P(("group", "col"), None),
        P(),
        P(("group", "col"), None),
        P("col", None),
        P(("group", "col"), None),
        P(("group", "col"), None),
        P("group", "col"),
        P("group"),
    )
    out_specs = (P("group", "col"), P("group"))
    return jax.shard_map(shards, mesh=mesh, in_specs=in_specs, out_specs=out_specs, check_vma=False)
```

```python
import functools

import jax
import jax.numpy as jnp
from jax import lax
from jax.experimental import pallas as pl
from jax.experimental.pallas import tpu as pltpu
from jax.sharding import PartitionSpec as P

NGRAM = 2
R_GRP = 8192
PAD = 8
VMEM_LIMIT = 56 * 1024 * 1024
learn_rate = 0.5

NT = (((1,), (1,)), ((), ()))
NN = (((1,), (0,)), ((), ()))


def slots_of(ngram_ids, groups):
    tok = ngram_ids.shape[0]
    ids = ngram_ids.reshape(-1)
    n = ids.shape[0]
    order = jnp.arange(n, dtype=jnp.int32)
    same = ids[:, None] == ids[None, :]
    leader = jnp.min(jnp.where(same, order[None, :], n), axis=1)
    lead = leader == order
    owner = ids // R_GRP
    before = lead[None, :] & (owner[:, None] == owner[None, :]) & (order[None, :] < leader[:, None])
    slot = jnp.sum(before.astype(jnp.int32), axis=1)
    places = jnp.arange(groups * tok, dtype=jnp.int32)
    rows = jnp.min(
        jnp.where(
            places[:, None] == (owner * tok + slot)[None, :], (ids - owner * R_GRP)[None, :], R_GRP
        ),
        axis=1,
    )
    mine = owner[None, :] == jnp.arange(groups, dtype=jnp.int32)[:, None]
    maps = jnp.where(mine, slot[None, :], -1).reshape(groups, tok, NGRAM)
    parts = [rows.reshape(groups, tok)] + [maps[:, :, j] for j in range(NGRAM)]
    return jnp.concatenate(parts, axis=1)


def product_kernel(pieces, first, last, columns, *refs):
    n = len(pieces)
    where, refs = refs[0], refs[1:]
    cot_own, cot_pair = refs[0], refs[1]
    ws = refs[2 : 2 + n]
    tok, deep = cot_own.shape
    depth = deep // 2
    if first:
        v_own, v_pair, ng, ss = refs[2 + n :]
        ng[...] = jnp.zeros_like(ng)
    else:
        held, gain, v_own, v_pair, ng, inner = refs[2 + n :]
        ng[...] = held[...]
    lanes = ng.shape[3]
    for (half, blocks), w in zip(pieces, ws):
        at = slice(half * depth, (half + 1) * depth)
        for k in range(0, len(blocks), 2):
            rows = w[k * lanes : (k + 2) * lanes, :]
            for part, cot in enumerate((cot_own, cot_pair)):
                p = lax.dot_general(cot[:, at], rows, NT, preferred_element_type=jnp.float32)
                for j in range(2):
                    ng[blocks[k + j], part] += p[:, j * lanes : (j + 1) * lanes]
    if first:
        for part, v in enumerate((v_own, v_pair)):

            def squares(j, total):
                x = v[:, pl.ds(pl.multiple_of(j * lanes, lanes), lanes)].astype(jnp.float32)
                return total + x * x

            ss[part] = lax.fori_loop(0, columns, squares, jnp.zeros((tok, lanes), jnp.float32))
    if last:
        for part, v in enumerate((v_own, v_pair)):

            def products(j, total):
                at = pl.ds(pl.multiple_of(where[j] * lanes, lanes), lanes)
                scaled = ng[j, part] * gain[:, at].astype(jnp.float32)
                ng[j, part] = scaled
                return total + scaled * v[:, at].astype(jnp.float32)

            inner[part] = lax.fori_loop(
                0, ng.shape[0], products, jnp.zeros((tok, lanes), jnp.float32)
            )


def finish_kernel(width, where, ng, ss, inner, other, v_own, v_pair, r_own, r_pair, out):
    tok, lanes = ng.shape[2:]
    core = lax.rem(where[0], 2)
    for part, (v, r) in enumerate(((v_own, r_own), (v_pair, r_pair))):
        square = jnp.sum(ss[part], axis=1, keepdims=True)
        inverse = lax.rsqrt(square / width + 1e-05)
        cubed = inverse * inverse * inverse
        mean = jnp.sum(inner[part] + other[1 - part], axis=1, keepdims=True) / width
        place = core if part == 0 else 1 - core

        def block(j, carry):
            at = pl.ds(pl.multiple_of(where[j] * lanes, lanes), lanes)
            values = v[:, at].astype(jnp.float32)
            total = inverse * ng[j, part] - values * cubed * mean + r[:, at].astype(jnp.float32)
            out[lax.div(where[j], 2), place] = total.astype(out.dtype)
            return carry

        lax.fori_loop(0, ng.shape[0], block, 0)


def vmem_call(kernel, n, out_shape, name, aliases=None):
    space = pl.BlockSpec(memory_space=pltpu.VMEM)
    return pl.pallas_call(
        kernel,
        in_specs=[pl.BlockSpec(memory_space=pltpu.SMEM)] + [space] * (n - 1),
        out_specs=jax.tree.map(lambda _: space, out_shape),
        out_shape=out_shape,
        input_output_aliases=aliases or {},
        compiler_params=pltpu.CompilerParams(vmem_limit_bytes=40 * 1024 * 1024),
        name=name,
    )


def shifted(value, inner_size, size, by):
    pairs = []
    for d in range(lax.axis_size("col")):
        low, high = d % inner_size, d // inner_size
        mid, top = high % size, high // size
        pairs.append((d, (top * size + (mid + by) % size) * inner_size + low))
    return lax.ppermute(value, "col", pairs)


def along(x, axis):
    inner_size = {"x": 2, "z": 8}[axis]
    left, right = shifted(x, inner_size, 4, 1), shifted(x, inner_size, 4, 3)
    return left, right


def token_grads(cot, w, v, r, gain, lanes, plan):
    columns = lax.axis_size("col")
    tok, width = v.shape
    depth = w.shape[1] // 2
    me = lax.axis_index("col")
    z, x, core = me // 8, (me // 2) % 4, me % 2
    where = jnp.stack(
        [
            (((z + 4 - dz) % 4) * 4 + (x + 4 - dx) % 4) * 2 + core
            for dz in range(4)
            for dx in range(4)
        ]
    ).astype(jnp.int32)
    cot_pair, v_pair, r_pair = (shifted(t, 1, 2, 1) for t in (cot, v, r))
    step = {"x": 2, "z": 8}
    firsts = []
    for half, axis in enumerate("xz"):
        own = w[:, half * depth : (half + 1) * depth]
        firsts.append((own, *along(own, axis)))
    lows = [jnp.concatenate([own, left]) for own, left, _ in firsts]
    low_sides = [along(lows[0], "z"), along(lows[1], "x")]
    highs = []
    for half, axis in enumerate("xz"):
        _, left, right = firsts[half]
        part = left.shape[0] // 2
        near = shifted(left[:part], step[axis], 4, 1)
        farther = shifted(right[part:], step[axis], 4, 3)
        highs.append(jnp.concatenate([near, farther, right]))
    high_sides = [along(highs[0], "z"), along(highs[1], "x")]
    far = [
        (shifted(low_sides[half][0], step[axis], 4, 1), shifted(high_sides[half][1], step[axis], 4, 3))
        for half, axis in enumerate("zx")
    ]

    def line(half, k, low=0, high=4):
        return (half, [k * 4 + j if half == 0 else j * 4 + k for j in range(low, high)])

    pieces, ws = [], []
    for half in range(2):
        low_set = (lows[half], *low_sides[half])
        high_set = (highs[half], *high_sides[half])
        for k, low, high in zip((0, 1, 3), low_set, high_set):
            pieces += [line(half, k, 0, 2), line(half, k, 2, 4)]
            ws += [low, high]
    product = jax.ShapeDtypeStruct((16, 2, tok, lanes), jnp.float32)
    stat = jax.ShapeDtypeStruct((2, tok, lanes), jnp.float32)
    plan, cot = lax.optimization_barrier((plan, cot))
    args = (where, cot, cot_pair, *ws, v, v_pair)
    ng, ss = vmem_call(
        functools.partial(product_kernel, pieces, True, False, columns),
        len(args),
        (product, stat),
        "product_near",
    )(*args)
    pieces, ws = [], []
    for half in range(2):
        for low, piece in ((0, far[half][0]), (2, far[half][1])):
            pieces.append(line(half, 2, low, low + 2))
            ws.append(piece)
    args = (where, cot, cot_pair, *ws, ng, gain.reshape(1, width), v, v_pair)
    scaled, inner = vmem_call(
        functools.partial(product_kernel, pieces, False, True, columns),
        len(args),
        (product, stat),
        "product_far",
        {len(args) - 4: 0},
    )(*args)
    other = shifted(inner, 1, 2, 1)
    args = (where, scaled, ss, inner, other, v, v_pair, r, r_pair)
    grads = vmem_call(
        functools.partial(finish_kernel, width),
        len(args),
        jax.ShapeDtypeStruct((16, 2, tok, lanes), jnp.bfloat16),
        "token_grads",
    )(*args)
    return grads, plan


def scatter_kernel(first, parts, per, batch, rows, counts, *refs):
    i = pl.program_id(0)
    n = len(parts)
    xs, maps = refs[:n], refs[n]
    if first:
        grad = refs[n + 1]
    else:
        held, grad = refs[n + 1], refs[n + 2]
    wide = refs[-1]
    tok, lanes = wide.shape[1], wide.shape[2]

    @pl.when(i == 0)
    def _():
        grad[...] = jnp.zeros_like(grad) if first else held[...]

    place = lax.broadcasted_iota(jnp.int32, (tok, tok), 0)

    def merge(x):
        for k in range(per):
            total = (place == maps[k, 0:1, :]).astype(jnp.float32)
            for j in range(1, NGRAM):
                total += (place == maps[k, j : j + 1, :]).astype(jnp.float32)
            wide[k] = (
                lax.dot_general(
                    total.astype(jnp.bfloat16), x[k], NN, preferred_element_type=jnp.float32
                )
                .astype(jnp.bfloat16)
                .astype(jnp.float32)
            )

    start = 0
    for p in range(n):
        pl.when((i >= start) & (i < start + parts[p]))(functools.partial(merge, xs[p]))
        start += parts[p]

    def block(k, carry):
        b = i * per + k

        def part(low, high):
            for base in range(low, high, batch):
                at = [rows[b * tok + base + s] for s in range(batch)]
                old = [grad[pl.ds(at[s], 1), :] for s in range(batch)]
                new = [old[s] + wide[k, pl.ds(base + s, 1), :] for s in range(batch)]
                for s in range(batch):
                    grad[pl.ds(at[s], 1), :] = new[s]

        part(0, tok // 2)

        @pl.when(counts[b] > tok // 2)
        def _():
            part(tok // 2, tok)

        return carry

    lax.fori_loop(0, per, block, 0)


def scattered(xs, maps, rows, counts, held):
    tok, lanes = xs[0].shape[1:]
    per = 8
    parts = [x.shape[0] // per for x in xs]
    starts = [sum(parts[:p]) for p in range(len(parts))]

    def piece(p):
        return lambda i, *_: (jnp.clip(i - starts[p], 0, parts[p] - 1), 0, 0)

    total = (R_GRP + PAD, lanes)
    in_specs = [pl.BlockSpec((per, tok, lanes), piece(p)) for p in range(len(xs))]
    in_specs.append(pl.BlockSpec((per, NGRAM, tok), lambda i, *_: (i, 0, 0)))
    args = [rows.reshape(-1), counts, *xs, maps]
    whole = lambda i, *_: (0, 0)
    if held is not None:
        in_specs.append(pl.BlockSpec(total, whole))
        args.append(held)
    return pl.pallas_call(
        functools.partial(scatter_kernel, held is None, parts, per, 16),
        grid_spec=pltpu.PrefetchScalarGridSpec(
            num_scalar_prefetch=2,
            grid=(sum(parts),),
            in_specs=in_specs,
            out_specs=pl.BlockSpec(total, whole),
            scratch_shapes=[pltpu.VMEM((per, tok, lanes), jnp.float32)],
        ),
        out_shape=jax.ShapeDtypeStruct(total, jnp.float32),
        input_output_aliases={} if held is None else {len(args) - 1: 0},
        compiler_params=pltpu.CompilerParams(
            dimension_semantics=("arbitrary",), vmem_limit_bytes=28 * 1024 * 1024
        ),
        cost_estimate=pl.CostEstimate(
            flops=1000000, bytes_accessed=900000 * sum(x.shape[0] for x in xs), transcendentals=0
        ),
        name="scatter_rows",
    )(*args)


def ring(x, by):
    n = lax.axis_size("group")
    return lax.ppermute(x, "group", [(d, (d + by) % n) for d in range(n)])


def col_sum(x):
    x = x + shifted(x, 1, 2, 1)
    for inner_size in (2, 8):
        first, second, third = (shifted(x, inner_size, 4, by) for by in (1, 3, 2))
        x = (x + third) + (first + second)
    return x


def shards(
    layer_input,
    norm_gain,
    keyvalue_cotangent,
    keyvalue_weight,
    residual_cotangent,
    ngram_ids,
    table,
    accumulator,
):
    groups, columns = lax.axis_size("group"), lax.axis_size("col")
    tok, width = layer_input.shape
    lanes = table.shape[1]
    def exchange(plan):
        sent = jnp.broadcast_to(plan[:, None, :], (groups, columns, plan.shape[1]))
        got = lax.all_to_all(
            sent.reshape(groups * columns, -1), ("group", "col"), 0, 0, tiled=True
        ).reshape(groups, columns, -1)
        me = lax.axis_index("group")
        order = [(me + by) % groups for by in (0, 3, 1, 2)]
        got = [lax.dynamic_index_in_dim(got, g, 0, False) for g in order]
        got = [got[0], jnp.concatenate(got[1:3]), got[3]]
        rows = [g[:, :tok] for g in got]
        maps = [g[:, tok:].reshape(-1, NGRAM, tok) for g in got]
        counts = [jnp.sum((r < R_GRP).astype(jnp.int32), axis=1) for r in rows]
        return rows, maps, counts

    grads, plan = token_grads(
        keyvalue_cotangent,
        keyvalue_weight,
        layer_input,
        residual_cotangent,
        norm_gain,
        lanes,
        slots_of(ngram_ids, groups),
    )
    planes = [[q * 2 + core for q in range(columns // 2)] for core in range(2)]
    own = lax.all_to_all(
        grads.reshape(columns // 2, 2 * tok, lanes),
        "col",
        0,
        0,
        axis_index_groups=planes,
        tiled=True,
    ).reshape(columns, tok, lanes)
    half = columns // 2
    low, high = own[:half], own[half:]
    low_left, high_right = ring(low, 1), ring(high, 3)
    high_left, low_right = ring(high, 1), ring(low, 3)
    rows, maps, counts = exchange(lax.optimization_barrier((plan, low, high))[0])
    grad = scattered((own,), maps[0], rows[0], counts[0], None)
    far = (ring(low_left, 1), ring(high_right, 3))
    near = (low_left, high_left, low_right, high_right)
    grad = scattered(near, maps[1], rows[1], counts[1], grad)
    grad = scattered(far, maps[2], rows[2], counts[2], grad)[:R_GRP]
    partial = jnp.sum(grad * grad, axis=1).reshape(-1, lanes)
    squares = col_sum(partial) / width
    new_accum = accumulator + squares.reshape(-1)
    new_table = table - learn_rate * grad * lax.rsqrt(new_accum)[:, None]
    return (new_table, new_accum)


def solution(mesh):
    in_specs = (
        P(("group", "col"), None),
        P(),
        P(("group", "col"), None),
        P("col", None),
        P(("group", "col"), None),
        P(("group", "col"), None),
        P("group", "col"),
        P("group"),
    )
    out_specs = (P("group", "col"), P("group"))
    return jax.shard_map(shards, mesh=mesh, in_specs=in_specs, out_specs=out_specs, check_vma=False)
```

```python
import functools

import jax
import jax.numpy as jnp
from jax import lax
from jax.experimental import pallas as pl
from jax.experimental.pallas import tpu as pltpu
from jax.sharding import PartitionSpec as P

NGRAM = 2
R_GRP = 8192
PAD = 8
VMEM_LIMIT = 56 * 1024 * 1024
learn_rate = 0.5

NT = (((1,), (1,)), ((), ()))
NN = (((1,), (0,)), ((), ()))


def slots_of(ngram_ids, groups):
    tok = ngram_ids.shape[0]
    ids = ngram_ids.reshape(-1)
    n = ids.shape[0]
    order = jnp.arange(n, dtype=jnp.int32)
    same = ids[:, None] == ids[None, :]
    leader = jnp.min(jnp.where(same, order[None, :], n), axis=1)
    lead = leader == order
    owner = ids // R_GRP
    before = lead[None, :] & (owner[:, None] == owner[None, :]) & (order[None, :] < leader[:, None])
    slot = jnp.sum(before.astype(jnp.int32), axis=1)
    places = jnp.arange(groups * tok, dtype=jnp.int32)
    rows = jnp.min(
        jnp.where(
            places[:, None] == (owner * tok + slot)[None, :], (ids - owner * R_GRP)[None, :], R_GRP
        ),
        axis=1,
    )
    mine = owner[None, :] == jnp.arange(groups, dtype=jnp.int32)[:, None]
    maps = jnp.where(mine, slot[None, :], -1).reshape(groups, tok, NGRAM)
    parts = [rows.reshape(groups, tok)] + [maps[:, :, j] for j in range(NGRAM)]
    return jnp.concatenate(parts, axis=1)


def product_kernel(pieces, first, last, columns, *refs):
    n = len(pieces)
    where, refs = refs[0], refs[1:]
    cot_own, cot_pair = refs[0], refs[1]
    ws = refs[2 : 2 + n]
    tok, deep = cot_own.shape
    depth = deep // 2
    if first:
        v_own, v_pair, ng, ss = refs[2 + n :]
        ng[...] = jnp.zeros_like(ng)
    else:
        held, gain, v_own, v_pair, ng, inner = refs[2 + n :]
        ng[...] = held[...]
    lanes = ng.shape[3]
    for (half, blocks), w in zip(pieces, ws):
        at = slice(half * depth, (half + 1) * depth)
        for k in range(0, len(blocks), 2):
            rows = w[k * lanes : (k + 2) * lanes, :]
            for part, cot in enumerate((cot_own, cot_pair)):
                p = lax.dot_general(cot[:, at], rows, NT, preferred_element_type=jnp.float32)
                for j in range(2):
                    ng[blocks[k + j], part] += p[:, j * lanes : (j + 1) * lanes]
    if first:
        for part, v in enumerate((v_own, v_pair)):

            def squares(j, total):
                x = v[:, pl.ds(pl.multiple_of(j * lanes, lanes), lanes)].astype(jnp.float32)
                return total + x * x

            ss[part] = lax.fori_loop(0, columns, squares, jnp.zeros((tok, lanes), jnp.float32))
    if last:
        for part, v in enumerate((v_own, v_pair)):

            def products(j, total):
                at = pl.ds(pl.multiple_of(where[j] * lanes, lanes), lanes)
                scaled = ng[j, part] * gain[:, at].astype(jnp.float32)
                ng[j, part] = scaled
                return total + scaled * v[:, at].astype(jnp.float32)

            inner[part] = lax.fori_loop(
                0, ng.shape[0], products, jnp.zeros((tok, lanes), jnp.float32)
            )


def finish_kernel(width, where, ng, ss, inner, other, v_own, v_pair, r_own, r_pair, out):
    tok, lanes = ng.shape[2:]
    core = lax.rem(where[0], 2)
    for part, (v, r) in enumerate(((v_own, r_own), (v_pair, r_pair))):
        square = jnp.sum(ss[part], axis=1, keepdims=True)
        inverse = lax.rsqrt(square / width + 1e-05)
        cubed = inverse * inverse * inverse
        mean = jnp.sum(inner[part] + other[1 - part], axis=1, keepdims=True) / width
        place = core if part == 0 else 1 - core

        def block(j, carry):
            at = pl.ds(pl.multiple_of(where[j] * lanes, lanes), lanes)
            values = v[:, at].astype(jnp.float32)
            total = inverse * ng[j, part] - values * cubed * mean + r[:, at].astype(jnp.float32)
            out[lax.div(where[j], 2), place] = total.astype(out.dtype)
            return carry

        lax.fori_loop(0, ng.shape[0], block, 0)


def vmem_call(kernel, n, out_shape, name, aliases=None):
    space = pl.BlockSpec(memory_space=pltpu.VMEM)
    return pl.pallas_call(
        kernel,
        in_specs=[pl.BlockSpec(memory_space=pltpu.SMEM)] + [space] * (n - 1),
        out_specs=jax.tree.map(lambda _: space, out_shape),
        out_shape=out_shape,
        input_output_aliases=aliases or {},
        compiler_params=pltpu.CompilerParams(vmem_limit_bytes=40 * 1024 * 1024),
        name=name,
    )


def shifted(value, inner_size, size, by):
    pairs = []
    for d in range(lax.axis_size("col")):
        low, high = d % inner_size, d // inner_size
        mid, top = high % size, high // size
        pairs.append((d, (top * size + (mid + by) % size) * inner_size + low))
    return lax.ppermute(value, "col", pairs)


def along(x, axis):
    inner_size = {"x": 2, "z": 8}[axis]
    left, right = shifted(x, inner_size, 4, 1), shifted(x, inner_size, 4, 3)
    return left, right


def token_grads(cot, w, v, r, gain, lanes, plan):
    columns = lax.axis_size("col")
    tok, width = v.shape
    depth = w.shape[1] // 2
    me = lax.axis_index("col")
    z, x, core = me // 8, (me // 2) % 4, me % 2
    where = jnp.stack(
        [
            (((z + 4 - dz) % 4) * 4 + (x + 4 - dx) % 4) * 2 + core
            for dz in range(4)
            for dx in range(4)
        ]
    ).astype(jnp.int32)
    cot_pair, v_pair, r_pair = (shifted(t, 1, 2, 1) for t in (cot, v, r))
    step = {"x": 2, "z": 8}
    firsts = []
    for half, axis in enumerate("xz"):
        own = w[:, half * depth : (half + 1) * depth]
        firsts.append((own, *along(own, axis), shifted(own, step[axis], 4, 2)))
    lows = [jnp.concatenate([own, left]) for own, left, _, _ in firsts]
    highs = [jnp.concatenate([farther, right]) for _, _, right, farther in firsts]
    low_sides = [along(lows[0], "z"), along(lows[1], "x")]
    high_sides = [along(highs[0], "z"), along(highs[1], "x")]
    far = [
        (shifted(low_sides[half][0], step[axis], 4, 1), shifted(high_sides[half][1], step[axis], 4, 3))
        for half, axis in enumerate("zx")
    ]

    def line(half, k, low=0, high=4):
        return (half, [k * 4 + j if half == 0 else j * 4 + k for j in range(low, high)])

    pieces, ws = [], []
    for half in range(2):
        low_set = (lows[half], *low_sides[half])
        high_set = (highs[half], *high_sides[half])
        for k, low, high in zip((0, 1, 3), low_set, high_set):
            pieces += [line(half, k, 0, 2), line(half, k, 2, 4)]
            ws += [low, high]
    product = jax.ShapeDtypeStruct((16, 2, tok, lanes), jnp.float32)
    stat = jax.ShapeDtypeStruct((2, tok, lanes), jnp.float32)
    plan, cot = lax.optimization_barrier((plan, cot))
    args = (where, cot, cot_pair, *ws, v, v_pair)
    ng, ss = vmem_call(
        functools.partial(product_kernel, pieces, True, False, columns),
        len(args),
        (product, stat),
        "product_near",
    )(*args)
    pieces, ws = [], []
    for half in range(2):
        for low, piece in ((0, far[half][0]), (2, far[half][1])):
            pieces.append(line(half, 2, low, low + 2))
            ws.append(piece)
    args = (where, cot, cot_pair, *ws, ng, gain.reshape(1, width), v, v_pair)
    scaled, inner = vmem_call(
        functools.partial(product_kernel, pieces, False, True, columns),
        len(args),
        (product, stat),
        "product_far",
        {len(args) - 4: 0},
    )(*args)
    other = shifted(inner, 1, 2, 1)
    args = (where, scaled, ss, inner, other, v, v_pair, r, r_pair)
    grads = vmem_call(
        functools.partial(finish_kernel, width),
        len(args),
        jax.ShapeDtypeStruct((16, 2, tok, lanes), jnp.bfloat16),
        "token_grads",
    )(*args)
    return grads, plan


def scatter_kernel(first, parts, index, per, batch, rows, counts, *refs):
    i = pl.program_id(0)
    n = len(parts)
    xs, maps = refs[:n], refs[n]
    if first:
        grad = refs[n + 1]
    else:
        held, grad = refs[n + 1], refs[n + 2]
    wide = refs[-1]
    tok, lanes = wide.shape[1], wide.shape[2]

    @pl.when(i == 0)
    def _():
        grad[...] = jnp.zeros_like(grad) if first else held[...]

    place = lax.broadcasted_iota(jnp.int32, (tok, tok), 0)

    def merge(x):
        for k in range(per):
            total = (place == maps[k, 0:1, :]).astype(jnp.float32)
            for j in range(1, NGRAM):
                total += (place == maps[k, j : j + 1, :]).astype(jnp.float32)
            wide[k] = (
                lax.dot_general(
                    total.astype(jnp.bfloat16), x[k], NN, preferred_element_type=jnp.float32
                )
                .astype(jnp.bfloat16)
                .astype(jnp.float32)
            )

    start = 0
    for p in range(n):
        pl.when((i >= start) & (i < start + parts[p]))(functools.partial(merge, xs[p]))
        start += parts[p]

    def block(k, carry):
        b = index(i) * per + k

        def part(low, high):
            for base in range(low, high, batch):
                at = [rows[b * tok + base + s] for s in range(batch)]
                old = [grad[pl.ds(at[s], 1), :] for s in range(batch)]
                new = [old[s] + wide[k, pl.ds(base + s, 1), :] for s in range(batch)]
                for s in range(batch):
                    grad[pl.ds(at[s], 1), :] = new[s]

        part(0, tok // 2)

        @pl.when(counts[b] > tok // 2)
        def _():
            part(tok // 2, tok)

        return carry

    lax.fori_loop(0, per, block, 0)


def scattered(xs, maps, rows, counts, held, skips=(0, 0)):
    tok, lanes = xs[0].shape[1:]
    per = 8
    parts = [x.shape[0] // per for x in xs]
    starts = [sum(parts[:p]) for p in range(len(parts))]

    def index(i):
        return i + jnp.where(i < parts[0], skips[0], skips[1])

    def piece(p):
        return lambda i, *_: (jnp.clip(i - starts[p], 0, parts[p] - 1), 0, 0)

    total = (R_GRP + PAD, lanes)
    in_specs = [pl.BlockSpec((per, tok, lanes), piece(p)) for p in range(len(xs))]
    in_specs.append(pl.BlockSpec((per, NGRAM, tok), lambda i, *_: (index(i), 0, 0)))
    args = [rows.reshape(-1), counts, *xs, maps]
    stays = pl.BlockSpec(memory_space=pltpu.VMEM)
    if held is not None:
        in_specs.append(stays)
        args.append(held)
    return pl.pallas_call(
        functools.partial(scatter_kernel, held is None, parts, index, per, 16),
        grid_spec=pltpu.PrefetchScalarGridSpec(
            num_scalar_prefetch=2,
            grid=(sum(parts),),
            in_specs=in_specs,
            out_specs=stays,
            scratch_shapes=[pltpu.VMEM((per, tok, lanes), jnp.float32)],
        ),
        out_shape=jax.ShapeDtypeStruct(total, jnp.float32),
        input_output_aliases={} if held is None else {len(args) - 1: 0},
        compiler_params=pltpu.CompilerParams(
            dimension_semantics=("arbitrary",), vmem_limit_bytes=20 * 1024 * 1024
        ),
        cost_estimate=pl.CostEstimate(
            flops=1000000, bytes_accessed=900000 * sum(x.shape[0] for x in xs), transcendentals=0
        ),
        name="scatter_rows",
    )(*args)


def ring(x, by):
    n = lax.axis_size("group")
    return lax.ppermute(x, "group", [(d, (d + by) % n) for d in range(n)])


def col_sum(x):
    x = x + shifted(x, 1, 2, 1)
    for inner_size in (2, 8):
        first, second, third = (shifted(x, inner_size, 4, by) for by in (1, 3, 2))
        x = (x + third) + (first + second)
    return x


def shards(
    layer_input,
    norm_gain,
    keyvalue_cotangent,
    keyvalue_weight,
    residual_cotangent,
    ngram_ids,
    table,
    accumulator,
):
    groups, columns = lax.axis_size("group"), lax.axis_size("col")
    tok, width = layer_input.shape
    lanes = table.shape[1]
    def exchange(plan):
        sent = jnp.broadcast_to(plan[:, None, :], (groups, columns, plan.shape[1]))
        got = lax.all_to_all(
            sent.reshape(groups * columns, -1), ("group", "col"), 0, 0, tiled=True
        ).reshape(groups, columns, -1)
        me = lax.axis_index("group")
        order = [(me + by) % groups for by in (0, 3, 1, 2)]
        got = [lax.dynamic_index_in_dim(got, g, 0, False) for g in order]
        got = [got[0], jnp.concatenate(got[1:3]), got[3]]
        rows = [g[:, :tok] for g in got]
        maps = [g[:, tok:].reshape(-1, NGRAM, tok) for g in got]
        counts = [jnp.sum((r < R_GRP).astype(jnp.int32), axis=1) for r in rows]
        return rows, maps, counts

    grads, plan = token_grads(
        keyvalue_cotangent,
        keyvalue_weight,
        layer_input,
        residual_cotangent,
        norm_gain,
        lanes,
        slots_of(ngram_ids, groups),
    )
    planes = [[q * 2 + core for q in range(columns // 2)] for core in range(2)]
    own = lax.all_to_all(
        grads.reshape(columns // 2, 2 * tok, lanes),
        "col",
        0,
        0,
        axis_index_groups=planes,
        tiled=True,
    ).reshape(columns, tok, lanes)
    half = columns // 2
    low, high = own[:half], own[half:]
    low_left, high_right = ring(low, 1), ring(high, 3)
    high_left, low_right = ring(high, 1), ring(low, 3)
    rows, maps, counts = exchange(lax.optimization_barrier((plan, low, high))[0])
    grad = scattered((own,), maps[0], rows[0], counts[0], None)
    far = (ring(low_left, 1), ring(high_right, 3))
    quarter = half // 8
    first, then = (low_left, high_right), (high_left, low_right)
    grad = scattered(first, maps[1], rows[1], counts[1], grad, (0, 2 * quarter))
    grad = scattered(then, maps[1], rows[1], counts[1], grad, (quarter, quarter))
    grad = scattered(far, maps[2], rows[2], counts[2], grad)[:R_GRP]
    partial = jnp.sum(grad * grad, axis=1).reshape(-1, lanes)
    squares = col_sum(partial) / width
    new_accum = accumulator + squares.reshape(-1)
    new_table = table - learn_rate * grad * lax.rsqrt(new_accum)[:, None]
    return (new_table, new_accum)


def solution(mesh):
    in_specs = (
        P(("group", "col"), None),
        P(),
        P(("group", "col"), None),
        P("col", None),
        P(("group", "col"), None),
        P(("group", "col"), None),
        P("group", "col"),
        P("group"),
    )
    out_specs = (P("group", "col"), P("group"))
    return jax.shard_map(shards, mesh=mesh, in_specs=in_specs, out_specs=out_specs, check_vma=False)
```

```python
import functools

import jax
import jax.numpy as jnp
from jax import lax
from jax.experimental import pallas as pl
from jax.experimental.pallas import tpu as pltpu
from jax.sharding import PartitionSpec as P

NGRAM = 2
R_GRP = 8192
PAD = 8
VMEM_LIMIT = 56 * 1024 * 1024
learn_rate = 0.5

NT = (((1,), (1,)), ((), ()))
NN = (((1,), (0,)), ((), ()))


def slots_of(ngram_ids, groups):
    tok = ngram_ids.shape[0]
    ids = ngram_ids.reshape(-1)
    n = ids.shape[0]
    order = jnp.arange(n, dtype=jnp.int32)
    same = ids[:, None] == ids[None, :]
    leader = jnp.min(jnp.where(same, order[None, :], n), axis=1)
    lead = leader == order
    owner = ids // R_GRP
    before = lead[None, :] & (owner[:, None] == owner[None, :]) & (order[None, :] < leader[:, None])
    slot = jnp.sum(before.astype(jnp.int32), axis=1)
    places = jnp.arange(groups * tok, dtype=jnp.int32)
    rows = jnp.min(
        jnp.where(
            places[:, None] == (owner * tok + slot)[None, :], (ids - owner * R_GRP)[None, :], R_GRP
        ),
        axis=1,
    )
    mine = owner[None, :] == jnp.arange(groups, dtype=jnp.int32)[:, None]
    maps = jnp.where(mine, slot[None, :], -1).reshape(groups, tok, NGRAM)
    parts = [rows.reshape(groups, tok)] + [maps[:, :, j] for j in range(NGRAM)]
    return jnp.concatenate(parts, axis=1)


def product_kernel(pieces, first, last, columns, *refs):
    n = len(pieces)
    where, refs = refs[0], refs[1:]
    cot_own, cot_pair = refs[0], refs[1]
    ws = refs[2 : 2 + n]
    tok, deep = cot_own.shape
    depth = deep // 2
    if first:
        v_own, v_pair, ng, ss = refs[2 + n :]
        ng[...] = jnp.zeros_like(ng)
    else:
        held, gain, v_own, v_pair, ng, inner = refs[2 + n :]
        ng[...] = held[...]
    lanes = ng.shape[3]
    for (half, blocks), w in zip(pieces, ws):
        at = slice(half * depth, (half + 1) * depth)
        for k in range(0, len(blocks), 2):
            rows = w[k * lanes : (k + 2) * lanes, :]
            for part, cot in enumerate((cot_own, cot_pair)):
                p = lax.dot_general(cot[:, at], rows, NT, preferred_element_type=jnp.float32)
                for j in range(2):
                    ng[blocks[k + j], part] += p[:, j * lanes : (j + 1) * lanes]
    if first:
        for part, v in enumerate((v_own, v_pair)):

            def squares(j, total):
                x = v[:, pl.ds(pl.multiple_of(j * lanes, lanes), lanes)].astype(jnp.float32)
                return total + x * x

            ss[part] = lax.fori_loop(0, columns, squares, jnp.zeros((tok, lanes), jnp.float32))
    if last:
        for part, v in enumerate((v_own, v_pair)):

            def products(j, total):
                at = pl.ds(pl.multiple_of(where[j] * lanes, lanes), lanes)
                scaled = ng[j, part] * gain[:, at].astype(jnp.float32)
                ng[j, part] = scaled
                return total + scaled * v[:, at].astype(jnp.float32)

            inner[part] = lax.fori_loop(
                0, ng.shape[0], products, jnp.zeros((tok, lanes), jnp.float32)
            )


def finish_kernel(width, where, ng, ss, inner, other, v_own, v_pair, r_own, r_pair, out):
    tok, lanes = ng.shape[2:]
    core = lax.rem(where[0], 2)
    for part, (v, r) in enumerate(((v_own, r_own), (v_pair, r_pair))):
        square = jnp.sum(ss[part], axis=1, keepdims=True)
        inverse = lax.rsqrt(square / width + 1e-05)
        cubed = inverse * inverse * inverse
        mean = jnp.sum(inner[part] + other[1 - part], axis=1, keepdims=True) / width
        place = core if part == 0 else 1 - core

        def block(j, carry):
            at = pl.ds(pl.multiple_of(where[j] * lanes, lanes), lanes)
            values = v[:, at].astype(jnp.float32)
            total = inverse * ng[j, part] - values * cubed * mean + r[:, at].astype(jnp.float32)
            out[lax.div(where[j], 2), place] = total.astype(out.dtype)
            return carry

        lax.fori_loop(0, ng.shape[0], block, 0)


def vmem_call(kernel, n, out_shape, name, aliases=None):
    space = pl.BlockSpec(memory_space=pltpu.VMEM)
    return pl.pallas_call(
        kernel,
        in_specs=[pl.BlockSpec(memory_space=pltpu.SMEM)] + [space] * (n - 1),
        out_specs=jax.tree.map(lambda _: space, out_shape),
        out_shape=out_shape,
        input_output_aliases=aliases or {},
        compiler_params=pltpu.CompilerParams(vmem_limit_bytes=40 * 1024 * 1024),
        name=name,
    )


def shifted(value, inner_size, size, by):
    pairs = []
    for d in range(lax.axis_size("col")):
        low, high = d % inner_size, d // inner_size
        mid, top = high % size, high // size
        pairs.append((d, (top * size + (mid + by) % size) * inner_size + low))
    return lax.ppermute(value, "col", pairs)


def along(x, axis):
    inner_size = {"x": 2, "z": 8}[axis]
    left, right = shifted(x, inner_size, 4, 1), shifted(x, inner_size, 4, 3)
    return left, right


def token_grads(cot, w, v, r, gain, lanes, plan):
    columns = lax.axis_size("col")
    tok, width = v.shape
    depth = w.shape[1] // 2
    me = lax.axis_index("col")
    z, x, core = me // 8, (me // 2) % 4, me % 2
    where = jnp.stack(
        [
            (((z + 4 - dz) % 4) * 4 + (x + 4 - dx) % 4) * 2 + core
            for dz in range(4)
            for dx in range(4)
        ]
    ).astype(jnp.int32)
    cot_pair, v_pair, r_pair = (shifted(t, 1, 2, 1) for t in (cot, v, r))
    step = {"x": 2, "z": 8}
    firsts = []
    for half, axis in enumerate("xz"):
        own = w[:, half * depth : (half + 1) * depth]
        firsts.append((own, *along(own, axis), shifted(own, step[axis], 4, 2)))
    lows = [jnp.concatenate([own, left]) for own, left, _, _ in firsts]
    highs = [jnp.concatenate([farther, right]) for _, _, right, farther in firsts]
    low_sides = [along(lows[0], "z"), along(lows[1], "x")]
    high_sides = [along(highs[0], "z"), along(highs[1], "x")]
    far = [
        (shifted(low_sides[half][0], step[axis], 4, 1), shifted(high_sides[half][1], step[axis], 4, 3))
        for half, axis in enumerate("zx")
    ]

    def line(half, k, low=0, high=4):
        return (half, [k * 4 + j if half == 0 else j * 4 + k for j in range(low, high)])

    pieces, ws = [], []
    for half in range(2):
        low_set = (lows[half], *low_sides[half])
        high_set = (highs[half], *high_sides[half])
        for k, low, high in zip((0, 1, 3), low_set, high_set):
            pieces += [line(half, k, 0, 2), line(half, k, 2, 4)]
            ws += [low, high]
    product = jax.ShapeDtypeStruct((16, 2, tok, lanes), jnp.float32)
    stat = jax.ShapeDtypeStruct((2, tok, lanes), jnp.float32)
    plan, cot = lax.optimization_barrier((plan, cot))
    args = (where, cot, cot_pair, *ws, v, v_pair)
    ng, ss = vmem_call(
        functools.partial(product_kernel, pieces, True, False, columns),
        len(args),
        (product, stat),
        "product_near",
    )(*args)
    pieces, ws = [], []
    for half in range(2):
        for low, piece in ((0, far[half][0]), (2, far[half][1])):
            pieces.append(line(half, 2, low, low + 2))
            ws.append(piece)
    args = (where, cot, cot_pair, *ws, ng, gain.reshape(1, width), v, v_pair)
    scaled, inner = vmem_call(
        functools.partial(product_kernel, pieces, False, True, columns),
        len(args),
        (product, stat),
        "product_far",
        {len(args) - 4: 0},
    )(*args)
    other = shifted(inner, 1, 2, 1)
    args = (where, scaled, ss, inner, other, v, v_pair, r, r_pair)
    grads = vmem_call(
        functools.partial(finish_kernel, width),
        len(args),
        jax.ShapeDtypeStruct((16, 2, tok, lanes), jnp.bfloat16),
        "token_grads",
    )(*args)
    return grads, plan


def scatter_kernel(first, parts, index, per, batch, rows, counts, *refs):
    i = pl.program_id(0)
    n = len(parts)
    xs, maps = refs[:n], refs[n]
    if first:
        grad = refs[n + 1]
    else:
        held, grad = refs[n + 1], refs[n + 2]
    wide = refs[-1]
    tok, lanes = wide.shape[1], wide.shape[2]

    @pl.when(i == 0)
    def _():
        grad[...] = jnp.zeros_like(grad) if first else held[...]

    place = lax.broadcasted_iota(jnp.int32, (tok, tok), 0)

    def merge(x):
        for k in range(per):
            total = (place == maps[k, 0:1, :]).astype(jnp.float32)
            for j in range(1, NGRAM):
                total += (place == maps[k, j : j + 1, :]).astype(jnp.float32)
            wide[k] = (
                lax.dot_general(
                    total.astype(jnp.bfloat16), x[k], NN, preferred_element_type=jnp.float32
                )
                .astype(jnp.bfloat16)
                .astype(jnp.float32)
            )

    start = 0
    for p in range(n):
        pl.when((i >= start) & (i < start + parts[p]))(functools.partial(merge, xs[p]))
        start += parts[p]

    def block(k, carry):
        b = index(i) * per + k

        def part(low, high):
            for base in range(low, high, batch):
                at = [rows[b * tok + base + s] for s in range(batch)]
                old = [grad[pl.ds(at[s], 1), :] for s in range(batch)]
                new = [old[s] + wide[k, pl.ds(base + s, 1), :] for s in range(batch)]
                for s in range(batch):
                    grad[pl.ds(at[s], 1), :] = new[s]

        part(0, tok // 2)

        @pl.when(counts[b] > tok // 2)
        def _():
            part(tok // 2, tok)

        return carry

    lax.fori_loop(0, per, block, 0)


def scattered(xs, maps, rows, counts, held, skips=(0, 0)):
    tok, lanes = xs[0].shape[1:]
    per = 16
    parts = [x.shape[0] // per for x in xs]
    starts = [sum(parts[:p]) for p in range(len(parts))]

    def index(i):
        return i + jnp.where(i < parts[0], skips[0], skips[1])

    def piece(p):
        return lambda i, *_: (jnp.clip(i - starts[p], 0, parts[p] - 1), 0, 0)

    total = (R_GRP + PAD, lanes)
    in_specs = [pl.BlockSpec((per, tok, lanes), piece(p)) for p in range(len(xs))]
    in_specs.append(pl.BlockSpec((per, NGRAM, tok), lambda i, *_: (index(i), 0, 0)))
    args = [rows.reshape(-1), counts, *xs, maps]
    stays = pl.BlockSpec(memory_space=pltpu.VMEM)
    if held is not None:
        in_specs.append(stays)
        args.append(held)
    return pl.pallas_call(
        functools.partial(scatter_kernel, held is None, parts, index, per, 16),
        grid_spec=pltpu.PrefetchScalarGridSpec(
            num_scalar_prefetch=2,
            grid=(sum(parts),),
            in_specs=in_specs,
            out_specs=stays,
            scratch_shapes=[pltpu.VMEM((per, tok, lanes), jnp.float32)],
        ),
        out_shape=jax.ShapeDtypeStruct(total, jnp.float32),
        input_output_aliases={} if held is None else {len(args) - 1: 0},
        compiler_params=pltpu.CompilerParams(
            dimension_semantics=("arbitrary",), vmem_limit_bytes=20 * 1024 * 1024
        ),
        cost_estimate=pl.CostEstimate(
            flops=1000000, bytes_accessed=900000 * sum(x.shape[0] for x in xs), transcendentals=0
        ),
        name="scatter_rows",
    )(*args)


def ring(x, by):
    n = lax.axis_size("group")
    return lax.ppermute(x, "group", [(d, (d + by) % n) for d in range(n)])


def col_sum(x):
    x = x + shifted(x, 1, 2, 1)
    for inner_size in (2, 8):
        first, second, third = (shifted(x, inner_size, 4, by) for by in (1, 3, 2))
        x = (x + third) + (first + second)
    return x


def shards(
    layer_input,
    norm_gain,
    keyvalue_cotangent,
    keyvalue_weight,
    residual_cotangent,
    ngram_ids,
    table,
    accumulator,
):
    groups, columns = lax.axis_size("group"), lax.axis_size("col")
    tok, width = layer_input.shape
    lanes = table.shape[1]
    def exchange(plan):
        sent = jnp.broadcast_to(plan[:, None, :], (groups, columns, plan.shape[1]))
        got = lax.all_to_all(
            sent.reshape(groups * columns, -1), ("group", "col"), 0, 0, tiled=True
        ).reshape(groups, columns, -1)
        me = lax.axis_index("group")
        order = [(me + by) % groups for by in (0, 3, 1, 2)]
        got = [lax.dynamic_index_in_dim(got, g, 0, False) for g in order]
        got = [got[0], jnp.concatenate(got[1:3]), got[3]]
        rows = [g[:, :tok] for g in got]
        maps = [g[:, tok:].reshape(-1, NGRAM, tok) for g in got]
        counts = [jnp.sum((r < R_GRP).astype(jnp.int32), axis=1) for r in rows]
        return rows, maps, counts

    grads, plan = token_grads(
        keyvalue_cotangent,
        keyvalue_weight,
        layer_input,
        residual_cotangent,
        norm_gain,
        lanes,
        slots_of(ngram_ids, groups),
    )
    planes = [[q * 2 + core for q in range(columns // 2)] for core in range(2)]
    own = lax.all_to_all(
        grads.reshape(columns // 2, 2 * tok, lanes),
        "col",
        0,
        0,
        axis_index_groups=planes,
        tiled=True,
    ).reshape(columns, tok, lanes)
    half = columns // 2
    low, high = own[:half], own[half:]
    low_left, high_right = ring(low, 1), ring(high, 3)
    high_left, low_right = ring(high, 1), ring(low, 3)
    rows, maps, counts = exchange(lax.optimization_barrier((plan, low, high))[0])
    grad = scattered((own,), maps[0], rows[0], counts[0], None)
    far = (ring(low_left, 1), ring(high_right, 3))
    quarter = half // 16
    first, then = (low_left, high_right), (high_left, low_right)
    grad = scattered(first, maps[1], rows[1], counts[1], grad, (0, 2 * quarter))
    grad = scattered(then, maps[1], rows[1], counts[1], grad, (quarter, quarter))
    grad = scattered(far, maps[2], rows[2], counts[2], grad)[:R_GRP]
    partial = jnp.sum(grad * grad, axis=1).reshape(-1, lanes)
    squares = col_sum(partial) / width
    new_accum = accumulator + squares.reshape(-1)
    new_table = table - learn_rate * grad * lax.rsqrt(new_accum)[:, None]
    return (new_table, new_accum)


def solution(mesh):
    in_specs = (
        P(("group", "col"), None),
        P(),
        P(("group", "col"), None),
        P("col", None),
        P(("group", "col"), None),
        P(("group", "col"), None),
        P("group", "col"),
        P("group"),
    )
    out_specs = (P("group", "col"), P("group"))
    return jax.shard_map(shards, mesh=mesh, in_specs=in_specs, out_specs=out_specs, check_vma=False)
```

```python
import functools

import jax
import jax.numpy as jnp
from jax import lax
from jax.experimental import pallas as pl
from jax.experimental.pallas import tpu as pltpu
from jax.sharding import PartitionSpec as P

NGRAM = 2
R_GRP = 8192
PAD = 8
VMEM_LIMIT = 56 * 1024 * 1024
learn_rate = 0.5

NT = (((1,), (1,)), ((), ()))
NN = (((1,), (0,)), ((), ()))


def slots_of(ngram_ids, groups):
    tok = ngram_ids.shape[0]
    ids = ngram_ids.reshape(-1)
    n = ids.shape[0]
    order = jnp.arange(n, dtype=jnp.int32)
    same = ids[:, None] == ids[None, :]
    leader = jnp.min(jnp.where(same, order[None, :], n), axis=1)
    lead = leader == order
    owner = ids // R_GRP
    before = lead[None, :] & (owner[:, None] == owner[None, :]) & (order[None, :] < leader[:, None])
    slot = jnp.sum(before.astype(jnp.int32), axis=1)
    places = jnp.arange(groups * tok, dtype=jnp.int32)
    rows = jnp.min(
        jnp.where(
            places[:, None] == (owner * tok + slot)[None, :], (ids - owner * R_GRP)[None, :], R_GRP
        ),
        axis=1,
    )
    mine = owner[None, :] == jnp.arange(groups, dtype=jnp.int32)[:, None]
    maps = jnp.where(mine, slot[None, :], -1).reshape(groups, tok, NGRAM)
    parts = [rows.reshape(groups, tok)] + [maps[:, :, j] for j in range(NGRAM)]
    return jnp.concatenate(parts, axis=1)


def product_kernel(pieces, first, last, columns, *refs):
    n = len(pieces)
    where, refs = refs[0], refs[1:]
    cot_own, cot_pair = refs[0], refs[1]
    ws = refs[2 : 2 + n]
    tok, deep = cot_own.shape
    depth = deep // 2
    if first:
        v_own, v_pair, ng, ss = refs[2 + n :]
        ng[...] = jnp.zeros_like(ng)
    else:
        held, gain, v_own, v_pair, ng, inner = refs[2 + n :]
        ng[...] = held[...]
    lanes = ng.shape[3]
    for (half, blocks), w in zip(pieces, ws):
        at = slice(half * depth, (half + 1) * depth)
        for k in range(0, len(blocks), 2):
            rows = w[k * lanes : (k + 2) * lanes, :]
            for part, cot in enumerate((cot_own, cot_pair)):
                p = lax.dot_general(cot[:, at], rows, NT, preferred_element_type=jnp.float32)
                for j in range(2):
                    ng[blocks[k + j], part] += p[:, j * lanes : (j + 1) * lanes]
    if first:
        for part, v in enumerate((v_own, v_pair)):

            def squares(j, total):
                x = v[:, pl.ds(pl.multiple_of(j * lanes, lanes), lanes)].astype(jnp.float32)
                return total + x * x

            ss[part] = lax.fori_loop(0, columns, squares, jnp.zeros((tok, lanes), jnp.float32))
    if last:
        for part, v in enumerate((v_own, v_pair)):

            def products(j, total):
                at = pl.ds(pl.multiple_of(where[j] * lanes, lanes), lanes)
                scaled = ng[j, part] * gain[:, at].astype(jnp.float32)
                ng[j, part] = scaled
                return total + scaled * v[:, at].astype(jnp.float32)

            inner[part] = lax.fori_loop(
                0, ng.shape[0], products, jnp.zeros((tok, lanes), jnp.float32)
            )


def finish_kernel(width, where, ng, ss, inner, other, v_own, v_pair, r_own, r_pair, out):
    tok, lanes = ng.shape[2:]
    core = lax.rem(where[0], 2)
    for part, (v, r) in enumerate(((v_own, r_own), (v_pair, r_pair))):
        square = jnp.sum(ss[part], axis=1, keepdims=True)
        inverse = lax.rsqrt(square / width + 1e-05)
        cubed = inverse * inverse * inverse
        mean = jnp.sum(inner[part] + other[1 - part], axis=1, keepdims=True) / width
        place = core if part == 0 else 1 - core

        def block(j, carry):
            at = pl.ds(pl.multiple_of(where[j] * lanes, lanes), lanes)
            values = v[:, at].astype(jnp.float32)
            total = inverse * ng[j, part] - values * cubed * mean + r[:, at].astype(jnp.float32)
            out[lax.div(where[j], 2), place] = total.astype(out.dtype)
            return carry

        lax.fori_loop(0, ng.shape[0], block, 0)


def vmem_call(kernel, n, out_shape, name, aliases=None):
    space = pl.BlockSpec(memory_space=pltpu.VMEM)
    return pl.pallas_call(
        kernel,
        in_specs=[pl.BlockSpec(memory_space=pltpu.SMEM)] + [space] * (n - 1),
        out_specs=jax.tree.map(lambda _: space, out_shape),
        out_shape=out_shape,
        input_output_aliases=aliases or {},
        compiler_params=pltpu.CompilerParams(vmem_limit_bytes=40 * 1024 * 1024),
        name=name,
    )


def shifted(value, inner_size, size, by):
    pairs = []
    for d in range(lax.axis_size("col")):
        low, high = d % inner_size, d // inner_size
        mid, top = high % size, high // size
        pairs.append((d, (top * size + (mid + by) % size) * inner_size + low))
    return lax.ppermute(value, "col", pairs)


def along(x, axis):
    inner_size = {"x": 2, "z": 8}[axis]
    left, right = shifted(x, inner_size, 4, 1), shifted(x, inner_size, 4, 3)
    return left, right


def token_grads(cot, w, v, r, gain, lanes, plan):
    columns = lax.axis_size("col")
    tok, width = v.shape
    depth = w.shape[1] // 2
    me = lax.axis_index("col")
    z, x, core = me // 8, (me // 2) % 4, me % 2
    where = jnp.stack(
        [
            (((z + 4 - dz) % 4) * 4 + (x + 4 - dx) % 4) * 2 + core
            for dz in range(4)
            for dx in range(4)
        ]
    ).astype(jnp.int32)
    cot_pair, v_pair, r_pair = (shifted(t, 1, 2, 1) for t in (cot, v, r))
    step = {"x": 2, "z": 8}
    firsts = []
    for half, axis in enumerate("xz"):
        own = w[:, half * depth : (half + 1) * depth]
        firsts.append((own, *along(own, axis), shifted(own, step[axis], 4, 2)))
    lows = [jnp.concatenate([own, left]) for own, left, _, _ in firsts]
    highs = [jnp.concatenate([farther, right]) for _, _, right, farther in firsts]
    low_sides = [along(lows[0], "z"), along(lows[1], "x")]
    high_sides = [along(highs[0], "z"), along(highs[1], "x")]
    far = [
        (shifted(low_sides[half][0], step[axis], 4, 1), shifted(high_sides[half][1], step[axis], 4, 3))
        for half, axis in enumerate("zx")
    ]

    def line(half, k, low=0, high=4):
        return (half, [k * 4 + j if half == 0 else j * 4 + k for j in range(low, high)])

    pieces, ws = [], []
    for half in range(2):
        low_set = (lows[half], *low_sides[half])
        high_set = (highs[half], *high_sides[half])
        for k, low, high in zip((0, 1, 3), low_set, high_set):
            pieces += [line(half, k, 0, 2), line(half, k, 2, 4)]
            ws += [low, high]
    product = jax.ShapeDtypeStruct((16, 2, tok, lanes), jnp.float32)
    stat = jax.ShapeDtypeStruct((2, tok, lanes), jnp.float32)
    plan, cot = lax.optimization_barrier((plan, cot))
    args = (where, cot, cot_pair, *ws, v, v_pair)
    ng, ss = vmem_call(
        functools.partial(product_kernel, pieces, True, False, columns),
        len(args),
        (product, stat),
        "product_near",
    )(*args)
    pieces, ws = [], []
    for half in range(2):
        for low, piece in ((0, far[half][0]), (2, far[half][1])):
            pieces.append(line(half, 2, low, low + 2))
            ws.append(piece)
    args = (where, cot, cot_pair, *ws, ng, gain.reshape(1, width), v, v_pair)
    scaled, inner = vmem_call(
        functools.partial(product_kernel, pieces, False, True, columns),
        len(args),
        (product, stat),
        "product_far",
        {len(args) - 4: 0},
    )(*args)
    other = shifted(inner, 1, 2, 1)
    args = (where, scaled, ss, inner, other, v, v_pair, r, r_pair)
    grads = vmem_call(
        functools.partial(finish_kernel, width),
        len(args),
        jax.ShapeDtypeStruct((16, 2, tok, lanes), jnp.bfloat16),
        "token_grads",
    )(*args)
    return grads, plan


def scatter_kernel(first, parts, index, per, batch, rows, counts, *refs):
    i = pl.program_id(0)
    n = len(parts)
    xs, maps = refs[:n], refs[n]
    if first:
        grad = refs[n + 1]
    else:
        held, grad = refs[n + 1], refs[n + 2]
    wide = refs[-1]
    tok, lanes = wide.shape[1], wide.shape[2]

    @pl.when(i == 0)
    def _():
        grad[...] = jnp.zeros_like(grad) if first else held[...]

    place = lax.broadcasted_iota(jnp.int32, (tok, tok), 0)

    def merge(x):
        for k in range(per):
            total = (place == maps[k, 0:1, :]).astype(jnp.float32)
            for j in range(1, NGRAM):
                total += (place == maps[k, j : j + 1, :]).astype(jnp.float32)
            wide[k] = (
                lax.dot_general(
                    total.astype(jnp.bfloat16), x[k], NN, preferred_element_type=jnp.float32
                )
                .astype(jnp.bfloat16)
                .astype(jnp.float32)
            )

    start = 0
    for p in range(n):
        pl.when((i >= start) & (i < start + parts[p]))(functools.partial(merge, xs[p]))
        start += parts[p]

    def block(k, carry):
        b = index(i) * per + k

        def part(low, high):
            for base in range(low, high, batch):
                at = [rows[b * tok + base + s] for s in range(batch)]
                old = [grad[pl.ds(at[s], 1), :] for s in range(batch)]
                new = [old[s] + wide[k, pl.ds(base + s, 1), :] for s in range(batch)]
                for s in range(batch):
                    grad[pl.ds(at[s], 1), :] = new[s]

        part(0, tok // 2)

        @pl.when(counts[b] > tok // 2)
        def _():
            part(tok // 2, tok)

        return carry

    lax.fori_loop(0, per, block, 0, unroll=2)


def scattered(xs, maps, rows, counts, held, skips=(0, 0)):
    tok, lanes = xs[0].shape[1:]
    per = 16
    parts = [x.shape[0] // per for x in xs]
    starts = [sum(parts[:p]) for p in range(len(parts))]

    def index(i):
        return i + jnp.where(i < parts[0], skips[0], skips[1])

    def piece(p):
        return lambda i, *_: (jnp.clip(i - starts[p], 0, parts[p] - 1), 0, 0)

    total = (R_GRP + PAD, lanes)
    in_specs = [pl.BlockSpec((per, tok, lanes), piece(p)) for p in range(len(xs))]
    in_specs.append(pl.BlockSpec((per, NGRAM, tok), lambda i, *_: (index(i), 0, 0)))
    args = [rows.reshape(-1), counts, *xs, maps]
    stays = pl.BlockSpec(memory_space=pltpu.VMEM)
    if held is not None:
        in_specs.append(stays)
        args.append(held)
    return pl.pallas_call(
        functools.partial(scatter_kernel, held is None, parts, index, per, 16),
        grid_spec=pltpu.PrefetchScalarGridSpec(
            num_scalar_prefetch=2,
            grid=(sum(parts),),
            in_specs=in_specs,
            out_specs=stays,
            scratch_shapes=[pltpu.VMEM((per, tok, lanes), jnp.float32)],
        ),
        out_shape=jax.ShapeDtypeStruct(total, jnp.float32),
        input_output_aliases={} if held is None else {len(args) - 1: 0},
        compiler_params=pltpu.CompilerParams(
            dimension_semantics=("arbitrary",), vmem_limit_bytes=20 * 1024 * 1024
        ),
        cost_estimate=pl.CostEstimate(
            flops=1000000, bytes_accessed=900000 * sum(x.shape[0] for x in xs), transcendentals=0
        ),
        name="scatter_rows",
    )(*args)


def ring(x, by):
    n = lax.axis_size("group")
    return lax.ppermute(x, "group", [(d, (d + by) % n) for d in range(n)])


def col_sum(x):
    x = x + shifted(x, 1, 2, 1)
    for inner_size in (2, 8):
        first, second, third = (shifted(x, inner_size, 4, by) for by in (1, 3, 2))
        x = (x + third) + (first + second)
    return x


def shards(
    layer_input,
    norm_gain,
    keyvalue_cotangent,
    keyvalue_weight,
    residual_cotangent,
    ngram_ids,
    table,
    accumulator,
):
    groups, columns = lax.axis_size("group"), lax.axis_size("col")
    tok, width = layer_input.shape
    lanes = table.shape[1]
    def exchange(plan):
        sent = jnp.broadcast_to(plan[:, None, :], (groups, columns, plan.shape[1]))
        got = lax.all_to_all(
            sent.reshape(groups * columns, -1), ("group", "col"), 0, 0, tiled=True
        ).reshape(groups, columns, -1)
        me = lax.axis_index("group")
        order = [(me + by) % groups for by in (0, 3, 1, 2)]
        got = [lax.dynamic_index_in_dim(got, g, 0, False) for g in order]
        got = [got[0], jnp.concatenate(got[1:3]), got[3]]
        rows = [g[:, :tok] for g in got]
        maps = [g[:, tok:].reshape(-1, NGRAM, tok) for g in got]
        counts = [jnp.sum((r < R_GRP).astype(jnp.int32), axis=1) for r in rows]
        return rows, maps, counts

    grads, plan = token_grads(
        keyvalue_cotangent,
        keyvalue_weight,
        layer_input,
        residual_cotangent,
        norm_gain,
        lanes,
        slots_of(ngram_ids, groups),
    )
    planes = [[q * 2 + core for q in range(columns // 2)] for core in range(2)]
    own = lax.all_to_all(
        grads.reshape(columns // 2, 2 * tok, lanes),
        "col",
        0,
        0,
        axis_index_groups=planes,
        tiled=True,
    ).reshape(columns, tok, lanes)
    half = columns // 2
    low, high = own[:half], own[half:]
    low_left, high_right = ring(low, 1), ring(high, 3)
    high_left, low_right = ring(high, 1), ring(low, 3)
    rows, maps, counts = exchange(lax.optimization_barrier((plan, low, high))[0])
    grad = scattered((own,), maps[0], rows[0], counts[0], None)
    far = (ring(low_left, 1), ring(high_right, 3))
    quarter = half // 16
    first, then = (low_left, high_right), (high_left, low_right)
    grad = scattered(first, maps[1], rows[1], counts[1], grad, (0, 2 * quarter))
    grad = scattered(then, maps[1], rows[1], counts[1], grad, (quarter, quarter))
    grad = scattered(far, maps[2], rows[2], counts[2], grad)[:R_GRP]
    partial = jnp.sum(grad * grad, axis=1).reshape(-1, lanes)
    squares = col_sum(partial) / width
    new_accum = accumulator + squares.reshape(-1)
    new_table = table - learn_rate * grad * lax.rsqrt(new_accum)[:, None]
    return (new_table, new_accum)


def solution(mesh):
    in_specs = (
        P(("group", "col"), None),
        P(),
        P(("group", "col"), None),
        P("col", None),
        P(("group", "col"), None),
        P(("group", "col"), None),
        P("group", "col"),
        P("group"),
    )
    out_specs = (P("group", "col"), P("group"))
    return jax.shard_map(shards, mesh=mesh, in_specs=in_specs, out_specs=out_specs, check_vma=False)
```
